32 devices in a mesh: groups: 2 (over y), dir: 2 (over x), space: 4 (over z), freq: 2 (over core).
Axes of the slice: x: 2, y: 2, z: 4, core: 2. Of those that a mesh axis runs over, the one named last changes fastest.
Arguments:
- spectrum: float32 [36, 32, 192, 256], P('dir', 'freq', ('groups', 'space')), parts along dimension 2, may hold values from 0.05 to 2
- land_mask: int32 [192, 256], P(('groups', 'space')), parts along dimension 0, may hold values 0 or 1
- depth_class: int32 [192, 256], P(('groups', 'space')), parts along dimension 0, may hold values from 0 to 7
- shift_count: int32 [192, 8], P(('groups', 'space')), parts along dimension 0, may hold values from -2 to 2
- turning: float32 [192, 256], P(('groups', 'space')), parts along dimension 0, may hold values from 0 to 1
- wind_rate: float32 [192, 256], P(('groups', 'space')), parts along dimension 0, may hold values from 0.02 to 0.2
- wind_angle: float32 [192, 256], P(('groups', 'space')), parts along dimension 0, may hold values from -3.140625 to 3.140625
- cfl: float32 [32], replicated, may hold values from 0.3 to 0.7
- freq_turn: float32 [32], replicated, may hold values from 0.3 to 1
- friction_table: float32 [8, 32], replicated, may hold values from 0.02 to 0.3
- transfer: float32 [1152, 1152], replicated, may hold values from -0.1875 to 0.1875
Outputs:
- evolved: float32 [36, 32, 192, 256], P('dir', 'freq', ('groups', 'space')), parts along dimension 2
The draws below stay inside these ranges and needn't reach their ends.
There are 2 independent parts, one for each index of `groups`. The reference program is written for one: setup_inputs(seed, part) draws one part's arguments, and reference() takes and returns one part's arrays. A program takes and returns all parts, laid end to end along the dimension named above; an argument that names none is the same for every part. Nothing has to cross between parts.
All inputs are finite; a program needn't handle non-finite values. No bound on the sum of `land_mask` on one device may be relied on, other than what follows from the above.
Results may differ from the reference program's by a relative error of at most 0.000071.
Values sent between devices are 32-bit elements; how exact they have to be, the bound alone decides.
A program may use at most 128 MiB of HBM per device.

```python
import math
import jax
import jax.numpy as jnp
from jax import lax

NDIR = 36
NFREQ = 32
NY = 256
TILE = 32
NCLASS = 8
REACH = 3
NBIN = 1152
NX = 96


def with_ends(drawn, rng, least, high):
    spot = [jax.random.randint(jax.random.fold_in(rng, axis), (), 0, length) for axis, length in enumerate(drawn.shape)]
    longest = drawn.shape.index(max(drawn.shape))
    next_to = spot[:longest] + [(spot[longest] + 1) % drawn.shape[longest]] + spot[longest + 1:]
    return drawn.at[tuple(spot)].set(least).at[tuple(next_to)].set(high)


def block_scale(rng, extent, pieces, least, high):
    factor_of = 1.0
    for dim, blocks in pieces:
        draws = jax.random.uniform(jax.random.fold_in(jax.random.fold_in(rng, 6), dim), (blocks,), jnp.float32, least / len(pieces), high / len(pieces))
        factor_of = factor_of * jnp.repeat(jnp.exp(draws), extent[dim] // blocks).reshape((-1,) + (1,) * (len(extent) - 1 - dim))
    return factor_of


def noise(key, extent, spread, limit, held_as=jnp.bfloat16):
    entries = jax.random.normal(key, extent, jnp.float32) * spread
    return jnp.minimum(jnp.maximum(entries, -limit), limit).astype(held_as)


def setup_inputs(seed: int = 0, part: int = 0) -> dict:
    splits = jax.random.split(jax.random.key(seed), 12)
    part_keys = jax.random.split(jax.random.fold_in(splits[11], part), 12)
    return {
        "spectrum": jnp.clip(jnp.exp(math.log(2.0) - 3.6888794 * jax.random.uniform(part_keys[0], (NDIR, NFREQ, NX, NY), jnp.float32) ** block_scale(part_keys[0], (NDIR, NFREQ, NX, NY), ((0, 2), (1, 2), (2, 4)), -0.2, 0.2)), 0.05, 2.0),
        "land_mask": with_ends((jax.random.randint(part_keys[1], (NX, NY), 0, 8) < 7).astype(jnp.int32), jax.random.fold_in(part_keys[1], 1), 0, 1),
        "depth_class": with_ends(jax.random.randint(part_keys[2], (NX, NY), 0, NCLASS), jax.random.fold_in(part_keys[2], 1), 0, NCLASS - 1).astype(jnp.int32),
        "shift_count": with_ends(jax.random.randint(part_keys[3], (NX, NY // TILE), 1 - REACH, REACH), jax.random.fold_in(part_keys[3], 1), 1 - REACH, REACH - 1).astype(jnp.int32),
        "turning": jnp.clip(1.0 * jax.random.uniform(part_keys[4], (NX, NY), jnp.float32) ** block_scale(part_keys[4], (NX, NY), ((0, 4),), -0.2, 0.2), 0.0, 1.0),
        "wind_rate": jnp.clip(jnp.exp(math.log(0.2) - 2.3025851 * jax.random.uniform(part_keys[5], (NX, NY), jnp.float32) ** block_scale(part_keys[5], (NX, NY), ((0, 4),), -0.2, 0.2)), 0.02, 0.2),
        "wind_angle": jnp.clip(jax.random.uniform(part_keys[6], (NX, NY), jnp.float32, -3.140625, 3.140625), -3.140625, 3.140625),
        "cfl": jnp.clip(jax.random.uniform(splits[7], (NFREQ,), jnp.float32, 0.3, 0.7), 0.3, 0.7),
        "freq_turn": jnp.clip(jnp.exp(jax.random.uniform(splits[8], (NFREQ,), jnp.float32, math.log(0.3), math.log(1.0))), 0.3, 1.0),
        "friction_table": jnp.clip(jnp.exp(jax.random.uniform(splits[9], (NCLASS, NFREQ), jnp.float32, math.log(0.02), math.log(0.3))), 0.02, 0.3),
        "transfer": noise(splits[10], (NBIN, NBIN), NBIN ** -0.5, 0.1875, jnp.float32),
    }


whitecap_coef = 0.01
nonlinear_coef = 0.5
small_eps = 1e-5


def frequencies(first, band_count):
    return 0.5 * jnp.power(1.07, (first + jnp.arange(band_count, dtype=jnp.int32)).astype(jnp.float32))


def propagate(masked, above_row, below_row, speed_x, speed_y):
    left_col = jnp.pad(masked, ((0, 0), (0, 0), (0, 0), (1, 0)))[:, :, :, :-1]
    right_col = jnp.pad(masked, ((0, 0), (0, 0), (0, 0), (0, 1)))[:, :, :, 1:]
    result = masked - jnp.maximum(speed_x, 0.0) * (masked - above_row)
    result = result - jnp.minimum(speed_x, 0.0) * (below_row - masked)
    result = result - jnp.maximum(speed_y, 0.0) * (masked - left_col)
    result = result - jnp.minimum(speed_y, 0.0) * (right_col - masked)
    return result


def turn_spectrum(padded, shifts, weights):
    dir_count = padded.shape[0] - 2 * REACH
    turned = jnp.zeros((dir_count,) + padded.shape[1:], padded.dtype)
    for offset in range(-REACH, REACH + 1):
        weight_off = jnp.where(shifts[None] == -offset, 1.0 - weights, 0.0) + jnp.where(shifts[None] == -offset - 1, weights, 0.0)
        turned = turned + weight_off[None] * padded[REACH + offset:REACH + offset + dir_count]
    return turned


def friction_lookup(depth_class, friction_table):
    onehot = (depth_class[None] == jnp.arange(friction_table.shape[0], dtype=jnp.int32)[:, None, None]).astype(jnp.float32)
    return jnp.einsum("cf,crn->frn", friction_table, onehot, precision=lax.Precision.HIGHEST)


def sources(spectrum, sigmas, angles, wind_rate, wind_angle, friction, transfer, sea_mask):
    bin_count = spectrum.shape[0] * spectrum.shape[1]
    sigma_wide = sigmas[None, :, None, None]
    energy = jnp.sum(spectrum, axis=(0, 1)) / bin_count
    first_moment = jnp.sum(spectrum * sigma_wide, axis=(0, 1)) / bin_count
    mean_sigma = first_moment / (energy + small_eps)
    steepness = energy * mean_sigma * mean_sigma
    alignment = jnp.maximum(jnp.cos(angles[:, None, None, None] - wind_angle[None, None]), 0.0)
    wind_input = wind_rate[None, None] * alignment * sigma_wide * spectrum
    whitecap = -whitecap_coef * (steepness * steepness)[None, None] * sigma_wide * spectrum
    bottom = -friction[None] * spectrum
    flattened = spectrum.reshape(bin_count, -1)
    mixed = lax.dot_general(transfer, flattened, (((0,), (0,)), ((), ())), precision=lax.Precision.HIGHEST, preferred_element_type=jnp.float32).reshape(spectrum.shape)
    nonlinear = nonlinear_coef * (energy * energy)[None, None] * mixed
    return sea_mask[None, None] * (spectrum + wind_input + whitecap + bottom + nonlinear)


def reference(spectrum, land_mask, depth_class, shift_count, turning, wind_rate, wind_angle, cfl, freq_turn, friction_table, transfer):
    sea_mask = (land_mask == 1).astype(jnp.float32)
    masked = spectrum * sea_mask[None, None]
    angles = 2.0 * math.pi * jnp.arange(NDIR, dtype=jnp.int32).astype(jnp.float32) / NDIR
    speed_x = cfl[None, :, None, None] * jnp.cos(angles)[:, None, None, None]
    speed_y = cfl[None, :, None, None] * jnp.sin(angles)[:, None, None, None]
    above_row = jnp.pad(masked, ((0, 0), (0, 0), (1, 0), (0, 0)))[:, :, :-1]
    below_row = jnp.pad(masked, ((0, 0), (0, 0), (0, 1), (0, 0)))[:, :, 1:]
    moved = propagate(masked, above_row, below_row, speed_x, speed_y) * sea_mask[None, None]
    shifts = jnp.repeat(shift_count, TILE, axis=1)
    weights = turning[None] * freq_turn[:, None, None]
    padded = jnp.concatenate([moved[-REACH:], moved, moved[:REACH]], axis=0)
    turned = turn_spectrum(padded, shifts, weights)
    sigmas = frequencies(0, NFREQ)
    friction = friction_lookup(depth_class, friction_table)
    return sources(turned, sigmas, angles, wind_rate, wind_angle, friction, transfer, sea_mask)
```

```python
import functools
import math

import jax
import jax.numpy as jnp
import numpy as np
from jax import lax
from jax.experimental import pallas as pl
from jax.experimental.pallas import tpu as pltpu
from jax.sharding import PartitionSpec as P

ROWS = 8
LANES = 128
MESH_ID = pl.DeviceIdType.MESH

whitecap_coef = 0.01
nonlinear_coef = 0.5
small_eps = 1e-05


def kernel(
    dir_groups,
    space_groups,
    spec_ref,
    land_ref,
    depth_ref,
    shift_ref,
    turning_ref,
    rate_ref,
    wind_ref,
    cfl_ref,
    turn_ref,
    fric_ref,
    cos_ref,
    sin_ref,
    sigma_ref,
    transfer_ref,
    out_ref,
    grid_buf,
    turned_buf,
    own_part,
    send_part,
    recv_part,
    out_buf,
    matrix,
    raw_matrix,
    edge_top,
    edge_bot,
    halo_up,
    halo_dn,
    sea_ref,
    shift_wide,
    coswind,
    sinwind,
    matrix_sem,
    halo_send,
    halo_recv,
    dir_send,
    dir_recv,
    part_send,
    part_recv,
    out_sem,
):
    me_dir = lax.axis_index("dir")
    me_space = lax.axis_index("space")
    me_freq = lax.axis_index("freq")
    other_freq = 1 - me_freq
    dir_total, freq_local = grid_buf.shape[1], grid_buf.shape[2]
    dir_local = dir_total // dir_groups
    bins = dir_local * freq_local
    row_count = out_ref.shape[1]
    col_count = out_ref.shape[2]
    tiles = row_count // ROWS
    halves = col_count // LANES
    chunks = tiles * halves
    class_count = fric_ref.shape[0]
    bin_total = transfer_ref.shape[2]
    dir_first = me_dir * dir_local
    freq_first = pl.multiple_of(me_freq * freq_local, 8)

    barrier = pltpu.get_barrier_semaphore()
    for j in range(1, dir_groups):
        pl.semaphore_signal(
            barrier, inc=1, device_id={"dir": lax.rem(me_dir + j, dir_groups)}, device_id_type=MESH_ID
        )
    pl.semaphore_signal(barrier, inc=1, device_id={"freq": other_freq}, device_id_type=MESH_ID)

    @pl.when(me_space > 0)
    def _():
        pl.semaphore_signal(barrier, inc=1, device_id={"space": me_space - 1}, device_id_type=MESH_ID)

    @pl.when(me_space < space_groups - 1)
    def _():
        pl.semaphore_signal(barrier, inc=1, device_id={"space": me_space + 1}, device_id_type=MESH_ID)

    matrix_copy = pltpu.make_async_copy(
        transfer_ref.at[:, pl.ds(freq_first, freq_local), :], raw_matrix, matrix_sem
    )
    matrix_copy.start()

    sea_ref[...] = jnp.where(land_ref[...] == 1, 1.0, 0.0)

    first_sea = sea_ref[pl.ds(0, ROWS), :]
    last_sea = sea_ref[pl.ds(row_count - ROWS, ROWS), :]

    def pack(b, carry):
        base = pl.multiple_of(b * row_count, ROWS)
        top = spec_ref[pl.ds(base, ROWS), :] * first_sea
        low = spec_ref[pl.ds(base + row_count - ROWS, ROWS), :] * last_sea
        edge_top[pl.ds(b, 1), :] = top[:1]
        edge_bot[pl.ds(b, 1), :] = low[ROWS - 1 :]
        return carry

    lax.fori_loop(0, bins, pack, 0, unroll=8)

    pl.semaphore_wait(
        barrier,
        dir_groups
        + (me_space > 0).astype(jnp.int32)
        + (me_space < space_groups - 1).astype(jnp.int32),
    )

    up_copy = pltpu.make_async_remote_copy(
        src_ref=edge_top,
        dst_ref=halo_dn,
        send_sem=halo_send.at[0],
        recv_sem=halo_recv.at[0],
        device_id={"space": jnp.maximum(me_space - 1, 0)},
        device_id_type=MESH_ID,
    )
    down_copy = pltpu.make_async_remote_copy(
        src_ref=edge_bot,
        dst_ref=halo_up,
        send_sem=halo_send.at[1],
        recv_sem=halo_recv.at[1],
        device_id={"space": jnp.minimum(me_space + 1, space_groups - 1)},
        device_id_type=MESH_ID,
    )

    @pl.when(me_space > 0)
    def _():
        up_copy.start()

    @pl.when(me_space < space_groups - 1)
    def _():
        down_copy.start()

    def dir_copy(c, j):
        region = grid_buf.at[c, pl.ds(dir_first, dir_local)]
        return pltpu.make_async_remote_copy(
            src_ref=region,
            dst_ref=region,
            send_sem=dir_send.at[c, j - 1],
            recv_sem=dir_recv.at[c, j - 1],
            device_id={"dir": lax.rem(me_dir + j, dir_groups)},
            device_id_type=MESH_ID,
        )

    row_id = lax.broadcasted_iota(jnp.int32, (ROWS, col_count), 0)
    col_id = lax.broadcasted_iota(jnp.int32, (ROWS, col_count), 1)

    def propagate(tile, place):
        sea = sea_ref[pl.ds(tile * ROWS, ROWS), :]
        if tile > 0:
            sea_prev = sea_ref[pl.ds(tile * ROWS - ROWS, ROWS), :]
        if tile < tiles - 1:
            sea_next = sea_ref[pl.ds(tile * ROWS + ROWS, ROWS), :]

        def per_dir(d, carry):
            cos_d = cos_ref[dir_first + d]
            sin_d = sin_ref[dir_first + d]

            def per_freq(f, inner):
                b = d * freq_local + f
                base = pl.multiple_of(b * row_count, ROWS)
                here = spec_ref[pl.ds(base + tile * ROWS, ROWS), :] * sea
                if tile > 0:
                    prev = spec_ref[pl.ds(base + (tile - 1) * ROWS, ROWS), :] * sea_prev
                    above = pltpu.roll(jnp.where(row_id == ROWS - 1, prev, here), 1, 0)
                else:
                    above = jnp.where(row_id == 0, halo_up[pl.ds(b, 1), :], pltpu.roll(here, 1, 0))
                if tile < tiles - 1:
                    later = spec_ref[pl.ds(base + (tile + 1) * ROWS, ROWS), :] * sea_next
                    below = pltpu.roll(jnp.where(row_id == 0, later, here), ROWS - 1, 0)
                else:
                    below = jnp.where(
                        row_id == ROWS - 1, halo_dn[pl.ds(b, 1), :], pltpu.roll(here, ROWS - 1, 0)
                    )
                left = jnp.where(col_id == 0, 0.0, pltpu.roll(here, 1, 1))
                right = jnp.where(col_id == col_count - 1, 0.0, pltpu.roll(here, col_count - 1, 1))
                speed = cfl_ref[freq_first + f]
                speed_x = speed * cos_d
                speed_y = speed * sin_d
                moved = here - jnp.maximum(speed_x, 0.0) * (here - above)
                moved = moved - jnp.minimum(speed_x, 0.0) * (below - here)
                moved = moved - jnp.maximum(speed_y, 0.0) * (here - left)
                moved = moved - jnp.minimum(speed_y, 0.0) * (right - here)
                moved = moved * sea
                for h in range(halves):
                    grid_buf[place * halves + h, dir_first + d, f] = moved[:, h * LANES : (h + 1) * LANES]
                return inner

            return lax.fori_loop(0, freq_local, per_freq, carry, unroll=4)

        lax.fori_loop(0, dir_local, per_dir, 0)
        for h in range(halves):
            for j in range(1, dir_groups):
                dir_copy(place * halves + h, j).start()

    for place in range(tiles - 2):
        propagate(place + 1, place)

    @pl.when(me_space > 0)
    def _():
        up_copy.wait_send()
        down_copy.wait_recv()

    @pl.when(me_space == 0)
    def _():
        halo_up[...] = jnp.zeros_like(halo_up)

    @pl.when(me_space < space_groups - 1)
    def _():
        down_copy.wait_send()
        up_copy.wait_recv()

    @pl.when(me_space == space_groups - 1)
    def _():
        halo_dn[...] = jnp.zeros_like(halo_dn)

    propagate(0, tiles - 2)
    propagate(tiles - 1, tiles - 1)

    coswind[...] = jnp.cos(wind_ref[...])
    sinwind[...] = jnp.sin(wind_ref[...])
    table_cols = lax.broadcasted_iota(jnp.int32, (row_count, col_count), 1)
    shift_tiles = shift_ref.shape[1]
    width = col_count // shift_tiles
    wide = jnp.zeros((row_count, col_count), jnp.int32)
    for s in range(shift_tiles):
        inside = (table_cols >= s * width) & (table_cols < (s + 1) * width)
        wide = jnp.where(inside, jnp.broadcast_to(shift_ref[:, s : s + 1], wide.shape), wide)
    shift_wide[...] = wide

    matrix_copy.wait()
    depth = dir_total * freq_local
    for m in range(bin_total // LANES):
        block = raw_matrix[:, :, m * LANES : (m + 1) * LANES].reshape(depth, LANES)
        high = block.astype(jnp.bfloat16).astype(jnp.float32)
        low = block - high
        turned_block = jnp.concatenate([high, low, high], axis=0).T.astype(jnp.bfloat16)
        for piece in range(LANES // freq_local):
            d, g = divmod(m * (LANES // freq_local) + piece, 2)
            matrix[g, pl.ds(d * freq_local, freq_local), :] = turned_block[
                piece * freq_local : (piece + 1) * freq_local
            ]

    def chunk(c, carry):
        place = c // halves
        half = c % halves
        tile = jnp.where(place < tiles - 2, place + 1, jnp.where(place == tiles - 2, 0, tiles - 1))
        rows = pl.ds(pl.multiple_of(tile * ROWS, ROWS), ROWS)
        cols = pl.ds(pl.multiple_of(half * LANES, LANES), LANES)
        for j in range(1, dir_groups):
            dir_copy(c, j).wait_recv()

        shift = shift_wide[rows, cols]
        turning = turning_ref[rows, cols]
        picks = [shift == k for k in range(-2, 2)]

        def refract(f, sums):
            weight = turning * turn_ref[freq_first + f]
            rest = 1.0 - weight
            moved = [grid_buf[c, d, f] for d in range(dir_total)]

            def shifted(d):
                result = moved[(d - 2) % dir_total]
                for k in (1, 0, -1, -2):
                    result = jnp.where(picks[k + 2], moved[(d - k) % dir_total], result)
                return result

            before = shifted(-1)
            total = jnp.zeros((ROWS, LANES), jnp.float32)
            for d in range(dir_total):
                now = shifted(d)
                turned = rest * now + weight * before
                turned_buf[pl.ds(pl.multiple_of((d * freq_local + f) * ROWS, ROWS), ROWS), :] = turned
                total = total + turned
                before = now
            return sums[0] + total, sums[1] + total * sigma_ref[freq_first + f]

        zero = jnp.zeros((ROWS, LANES), jnp.float32)
        energy, moment = lax.fori_loop(0, freq_local, refract, (zero, zero))
        send_part[pl.ds(bins * ROWS, ROWS), :] = energy
        send_part[pl.ds((bins + 1) * ROWS, ROWS), :] = moment

        mine = pl.ds(pl.multiple_of(dir_first * freq_local, 16), bins)

        def mix(pair, inner):
            first = turned_buf[pl.ds(2 * pair, depth, stride=ROWS), :]
            second = turned_buf[pl.ds(2 * pair + 1, depth, stride=ROWS), :]
            both = jnp.concatenate([first, second], axis=1)
            high = both.astype(jnp.bfloat16)
            low = (both - high.astype(jnp.float32)).astype(jnp.bfloat16)
            right = jnp.concatenate([high, high, low], axis=0)
            left = jnp.concatenate([matrix[me_freq, mine, :], matrix[other_freq, mine, :]], axis=0)
            part = jnp.dot(left, right, preferred_element_type=jnp.float32)
            own_part[pl.ds(2 * pair, bins, stride=ROWS), :] = part[:bins, :LANES]
            own_part[pl.ds(2 * pair + 1, bins, stride=ROWS), :] = part[:bins, LANES:]
            send_part[pl.ds(2 * pair, bins, stride=ROWS), :] = part[bins:, :LANES]
            send_part[pl.ds(2 * pair + 1, bins, stride=ROWS), :] = part[bins:, LANES:]
            return inner

        lax.fori_loop(0, ROWS // 2, mix, 0)
        swap = pltpu.make_async_remote_copy(
            src_ref=send_part,
            dst_ref=recv_part.at[c],
            send_sem=part_send.at[c],
            recv_sem=part_recv.at[c],
            device_id={"freq": other_freq},
            device_id_type=MESH_ID,
        )
        swap.start()
        swap.wait()

        sea = sea_ref[rows, cols]
        energy = (energy + recv_part[c, pl.ds(bins * ROWS, ROWS), :]) / bin_total
        moment = (moment + recv_part[c, pl.ds((bins + 1) * ROWS, ROWS), :]) / bin_total
        mean_sigma = moment / (energy + small_eps)
        steepness = energy * mean_sigma * mean_sigma
        white = whitecap_coef * (steepness * steepness)
        nonlinear = sea * (nonlinear_coef * (energy * energy))
        rate = sea * rate_ref[rows, cols]
        cos_w = coswind[rows, cols]
        sin_w = sinwind[rows, cols]
        classes = depth_ref[rows, cols]

        def source(f, inner):
            sigma = sigma_ref[freq_first + f]
            friction = jnp.full((ROWS, LANES), fric_ref[0, freq_first + f], jnp.float32)
            for k in range(1, class_count):
                friction = jnp.where(classes == k, fric_ref[k, freq_first + f], friction)
            keep = sea * (1.0 - white * sigma - friction)
            grow = rate * sigma
            for d in range(dir_local):
                at = pl.ds(pl.multiple_of((d * freq_local + f) * ROWS, ROWS), ROWS)
                whole = pl.ds(pl.multiple_of(((dir_first + d) * freq_local + f) * ROWS, ROWS), ROWS)
                align = jnp.maximum(cos_ref[dir_first + d] * cos_w + sin_ref[dir_first + d] * sin_w, 0.0)
                mixed = own_part[at, :] + recv_part[c, at, :]
                out_buf[c, d * freq_local + f] = (
                    turned_buf[whole, :] * (keep + grow * align) + nonlinear * mixed
                )
            return inner

        lax.fori_loop(0, freq_local, source, 0)
        out_copy(c, rows, cols).start()
        return carry

    def out_copy(c, rows, cols):
        return pltpu.make_async_copy(out_buf.at[c], out_ref.at[:, rows, cols], out_sem.at[c])

    lax.fori_loop(0, chunks, chunk, 0)

    def finish(c, carry):
        for j in range(1, dir_groups):
            dir_copy(c, j).wait_send()
        out_copy(c, pl.ds(0, ROWS), pl.ds(0, LANES)).wait()
        return carry

    lax.fori_loop(0, chunks, finish, 0)


def shards(
    dir_groups,
    space_groups,
    spectrum,
    land_mask,
    depth_class,
    shift_count,
    turning,
    wind_rate,
    wind_angle,
    cfl,
    freq_turn,
    friction_table,
    transfer,
):
    dir_local, freq_local, row_count, col_count = spectrum.shape
    bins = dir_local * freq_local
    dir_total = dir_local * dir_groups
    freq_total = cfl.shape[0]
    angles = 2.0 * math.pi * np.arange(dir_total) / dir_total
    cosines = jnp.asarray(np.cos(angles), jnp.float32)
    sines = jnp.asarray(np.sin(angles), jnp.float32)
    sigmas = jnp.asarray(0.5 * np.power(1.07, np.arange(freq_total)), jnp.float32)
    chunks = (row_count // ROWS) * (col_count // LANES)
    depth = dir_total * freq_local
    peers = max(dir_groups - 1, 1)
    vmem = pl.BlockSpec(memory_space=pltpu.VMEM)
    smem = pl.BlockSpec(memory_space=pltpu.SMEM)
    anywhere = pl.BlockSpec(memory_space=pl.ANY)
    f32 = jnp.float32
    evolved = pl.pallas_call(
        functools.partial(kernel, dir_groups, space_groups),
        out_shape=jax.ShapeDtypeStruct((bins, row_count, col_count), f32),
        in_specs=[vmem] * 7 + [smem] * 6 + [anywhere],
        out_specs=anywhere,
        scratch_shapes=[
            pltpu.VMEM((chunks, dir_total, freq_local, ROWS, LANES), f32),
            pltpu.VMEM((depth * ROWS, LANES), f32),
            pltpu.VMEM((bins * ROWS, LANES), f32),
            pltpu.VMEM(((bins + 2) * ROWS, LANES), f32),
            pltpu.VMEM((chunks, (bins + 2) * ROWS, LANES), f32),
            pltpu.VMEM((chunks, bins, ROWS, LANES), f32),
            pltpu.VMEM((2, depth, 3 * depth), jnp.bfloat16),
            pltpu.VMEM((dir_total, freq_local, transfer.shape[1]), f32),
            pltpu.VMEM((bins, col_count), f32),
            pltpu.VMEM((bins, col_count), f32),
            pltpu.VMEM((bins, col_count), f32),
            pltpu.VMEM((bins, col_count), f32),
            pltpu.VMEM((row_count, col_count), f32),
            pltpu.VMEM((row_count, col_count), jnp.int32),
            pltpu.VMEM((row_count, col_count), f32),
            pltpu.VMEM((row_count, col_count), f32),
            pltpu.SemaphoreType.DMA,
            pltpu.SemaphoreType.DMA((2,)),
            pltpu.SemaphoreType.DMA((2,)),
            pltpu.SemaphoreType.DMA((chunks, peers)),
            pltpu.SemaphoreType.DMA((chunks, peers)),
            pltpu.SemaphoreType.DMA((chunks,)),
            pltpu.SemaphoreType.DMA((chunks,)),
            pltpu.SemaphoreType.DMA((chunks,)),
        ],
        compiler_params=pltpu.CompilerParams(
            collective_id=0, has_side_effects=True, vmem_limit_bytes=60 * 1024 * 1024
        ),
        name="wave_step",
    )(
        spectrum.reshape(bins * row_count, col_count),
        land_mask,
        depth_class,
        shift_count,
        turning,
        wind_rate,
        wind_angle,
        cfl,
        freq_turn,
        friction_table,
        cosines,
        sines,
        sigmas,
        transfer.reshape(dir_total, freq_total, transfer.shape[1]),
    )
    return evolved.reshape(spectrum.shape)


def solution(mesh):
    points = P(("groups", "space"), None)
    in_specs = (P("dir", "freq", ("groups", "space"), None),) + (points,) * 6 + (P(),) * 4
    return jax.shard_map(
        functools.partial(shards, mesh.shape["dir"], mesh.shape["space"]),
        mesh=mesh,
        in_specs=in_specs,
        out_specs=P("dir", "freq", ("groups", "space"), None),
        check_vma=False,
    )
```

```python
import functools
import math

import jax
import jax.numpy as jnp
import numpy as np
from jax import lax
from jax.experimental import pallas as pl
from jax.experimental.pallas import tpu as pltpu
from jax.sharding import PartitionSpec as P

ROWS = 8
LANES = 128
MESH_ID = pl.DeviceIdType.MESH

whitecap_coef = 0.01
nonlinear_coef = 0.5
small_eps = 1e-05


def kernel(
    dir_groups,
    space_groups,
    spectrum_ref,
    land_ref,
    depth_ref,
    shift_ref,
    turning_ref,
    rate_ref,
    wind_ref,
    cfl_ref,
    turn_ref,
    fric_ref,
    cos_ref,
    sin_ref,
    sigma_ref,
    transfer_ref,
    out_ref,
    spec_ref,
    grid_buf,
    turned_buf,
    own_part,
    send_part,
    recv_part,
    matrix,
    raw_matrix,
    edge_top,
    edge_bot,
    halo_up,
    halo_dn,
    sea_ref,
    shift_wide,
    coswind,
    sinwind,
    spec_sem,
    matrix_sem,
    halo_send,
    halo_recv,
    dir_send,
    dir_recv,
    part_send,
    part_recv,
):
    me_dir = lax.axis_index("dir")
    me_space = lax.axis_index("space")
    me_freq = lax.axis_index("freq")
    other_freq = 1 - me_freq
    dir_total, freq_local = grid_buf.shape[1], grid_buf.shape[2]
    dir_local = dir_total // dir_groups
    bins = dir_local * freq_local
    row_count = out_ref.shape[1]
    col_count = out_ref.shape[2]
    tiles = row_count // ROWS
    halves = col_count // LANES
    chunks = tiles * halves
    class_count = fric_ref.shape[0]
    bin_total = transfer_ref.shape[2]
    dir_first = me_dir * dir_local
    freq_first = pl.multiple_of(me_freq * freq_local, 8)

    barrier = pltpu.get_barrier_semaphore()
    for j in range(1, dir_groups):
        pl.semaphore_signal(
            barrier, inc=1, device_id={"dir": lax.rem(me_dir + j, dir_groups)}, device_id_type=MESH_ID
        )
    pl.semaphore_signal(barrier, inc=1, device_id={"freq": other_freq}, device_id_type=MESH_ID)

    @pl.when(me_space > 0)
    def _():
        pl.semaphore_signal(barrier, inc=1, device_id={"space": me_space - 1}, device_id_type=MESH_ID)

    @pl.when(me_space < space_groups - 1)
    def _():
        pl.semaphore_signal(barrier, inc=1, device_id={"space": me_space + 1}, device_id_type=MESH_ID)

    def spec_copy(d):
        piece = pl.ds(pl.multiple_of(d * freq_local * row_count, ROWS), freq_local * row_count)
        return pltpu.make_async_copy(spectrum_ref.at[piece], spec_ref.at[piece], spec_sem.at[d])

    def start_copy(d, carry):
        spec_copy(d).start()
        return carry

    lax.fori_loop(0, dir_local, start_copy, 0)
    matrix_copy = pltpu.make_async_copy(
        transfer_ref.at[:, pl.ds(freq_first, freq_local), :], raw_matrix, matrix_sem
    )
    matrix_copy.start()

    sea_ref[...] = jnp.where(land_ref[...] == 1, 1.0, 0.0)

    first_sea = sea_ref[pl.ds(0, ROWS), :]
    last_sea = sea_ref[pl.ds(row_count - ROWS, ROWS), :]

    def pack(b):
        base = pl.multiple_of(b * row_count, ROWS)
        top = spec_ref[pl.ds(base, ROWS), :] * first_sea
        low = spec_ref[pl.ds(base + row_count - ROWS, ROWS), :] * last_sea
        edge_top[pl.ds(b, 1), :] = top[:1]
        edge_bot[pl.ds(b, 1), :] = low[ROWS - 1 :]

    pl.semaphore_wait(
        barrier,
        dir_groups
        + (me_space > 0).astype(jnp.int32)
        + (me_space < space_groups - 1).astype(jnp.int32),
    )

    up_copy = pltpu.make_async_remote_copy(
        src_ref=edge_top,
        dst_ref=halo_dn,
        send_sem=halo_send.at[0],
        recv_sem=halo_recv.at[0],
        device_id={"space": jnp.maximum(me_space - 1, 0)},
        device_id_type=MESH_ID,
    )
    down_copy = pltpu.make_async_remote_copy(
        src_ref=edge_bot,
        dst_ref=halo_up,
        send_sem=halo_send.at[1],
        recv_sem=halo_recv.at[1],
        device_id={"space": jnp.minimum(me_space + 1, space_groups - 1)},
        device_id_type=MESH_ID,
    )

    def dir_copy(c, j, first=0, count=dir_local):
        region = grid_buf.at[c, pl.ds(dir_first + first, count)]
        return pltpu.make_async_remote_copy(
            src_ref=region,
            dst_ref=region,
            send_sem=dir_send.at[c, j - 1],
            recv_sem=dir_recv.at[c, j - 1],
            device_id={"dir": lax.rem(me_dir + j, dir_groups)},
            device_id_type=MESH_ID,
        )

    row_id = lax.broadcasted_iota(jnp.int32, (ROWS, col_count), 0)
    col_id = lax.broadcasted_iota(jnp.int32, (ROWS, col_count), 1)

    def propagate(tile, place):
        sea = sea_ref[pl.ds(tile * ROWS, ROWS), :]
        if tile > 0:
            sea_prev = sea_ref[pl.ds(tile * ROWS - ROWS, ROWS), :]
        if tile < tiles - 1:
            sea_next = sea_ref[pl.ds(tile * ROWS + ROWS, ROWS), :]

        def per_dir(d, carry):
            if place == 0:
                spec_copy(d).wait()
            cos_d = cos_ref[dir_first + d]
            sin_d = sin_ref[dir_first + d]

            def per_freq(f, inner):
                b = d * freq_local + f
                if place == 0:
                    pack(b)
                base = pl.multiple_of(b * row_count, ROWS)
                here = spec_ref[pl.ds(base + tile * ROWS, ROWS), :] * sea
                if tile > 0:
                    prev = spec_ref[pl.ds(base + (tile - 1) * ROWS, ROWS), :] * sea_prev
                    above = pltpu.roll(jnp.where(row_id == ROWS - 1, prev, here), 1, 0)
                else:
                    above = jnp.where(row_id == 0, halo_up[pl.ds(b, 1), :], pltpu.roll(here, 1, 0))
                if tile < tiles - 1:
                    later = spec_ref[pl.ds(base + (tile + 1) * ROWS, ROWS), :] * sea_next
                    below = pltpu.roll(jnp.where(row_id == 0, later, here), ROWS - 1, 0)
                else:
                    below = jnp.where(
                        row_id == ROWS - 1, halo_dn[pl.ds(b, 1), :], pltpu.roll(here, ROWS - 1, 0)
                    )
                left = jnp.where(col_id == 0, 0.0, pltpu.roll(here, 1, 1))
                right = jnp.where(col_id == col_count - 1, 0.0, pltpu.roll(here, col_count - 1, 1))
                speed = cfl_ref[freq_first + f]
                speed_x = speed * cos_d
                speed_y = speed * sin_d
                moved = here - jnp.maximum(speed_x, 0.0) * (here - above)
                moved = moved - jnp.minimum(speed_x, 0.0) * (below - here)
                moved = moved - jnp.maximum(speed_y, 0.0) * (here - left)
                moved = moved - jnp.minimum(speed_y, 0.0) * (right - here)
                moved = moved * sea
                for h in range(halves):
                    grid_buf[place * halves + h, dir_first + d, f] = moved[:, h * LANES : (h + 1) * LANES]
                return inner

            lax.fori_loop(0, freq_local, per_freq, 0, unroll=4)
            if place == 0:
                for h in range(halves):
                    for j in range(1, dir_groups):
                        dir_copy(h, j, d, 1).start()
            return carry

        lax.fori_loop(0, dir_local, per_dir, 0)
        if place > 0:
            for h in range(halves):
                for j in range(1, dir_groups):
                    dir_copy(place * halves + h, j).start()

    for place in range(tiles - 2):
        propagate(place + 1, place)

    @pl.when(me_space > 0)
    def _():
        up_copy.start()

    @pl.when(me_space < space_groups - 1)
    def _():
        down_copy.start()

    @pl.when(me_space > 0)
    def _():
        up_copy.wait_send()
        down_copy.wait_recv()

    @pl.when(me_space == 0)
    def _():
        halo_up[...] = jnp.zeros_like(halo_up)

    @pl.when(me_space < space_groups - 1)
    def _():
        down_copy.wait_send()
        up_copy.wait_recv()

    @pl.when(me_space == space_groups - 1)
    def _():
        halo_dn[...] = jnp.zeros_like(halo_dn)

    propagate(0, tiles - 2)
    propagate(tiles - 1, tiles - 1)

    coswind[...] = jnp.cos(wind_ref[...])
    sinwind[...] = jnp.sin(wind_ref[...])
    shift_tiles = shift_ref.shape[0]
    width = col_count // shift_tiles
    tile_of = lax.broadcasted_iota(jnp.int32, (shift_tiles, col_count), 1) // width
    tile_id = lax.broadcasted_iota(jnp.int32, (shift_tiles, col_count), 0)
    shift_wide[...] = lax.dot_general(
        shift_ref[...].astype(jnp.float32),
        (tile_of == tile_id).astype(jnp.float32),
        (((0,), (0,)), ((), ())),
        preferred_element_type=jnp.float32,
    ).astype(jnp.int32)

    matrix_copy.wait()
    depth = dir_total * freq_local
    for m in range(bin_total // LANES):
        block = raw_matrix[:, :, m * LANES : (m + 1) * LANES].reshape(depth, LANES)
        high = block.astype(jnp.bfloat16).astype(jnp.float32)
        low = block - high
        turned_block = jnp.concatenate([high, low, high], axis=0).T.astype(jnp.bfloat16)
        for piece in range(LANES // freq_local):
            d, g = divmod(m * (LANES // freq_local) + piece, 2)
            matrix[g, pl.ds(d * freq_local, freq_local), :] = turned_block[
                piece * freq_local : (piece + 1) * freq_local
            ]

    middle = (dir_local + 1) // 2
    piece_ends = ((0, middle), (middle, dir_local))

    def chunk(c, carry):
        slot = c % 2
        place = c // halves
        half = c % halves
        tile = jnp.where(place < tiles - 2, place + 1, jnp.where(place == tiles - 2, 0, tiles - 1))
        rows = pl.ds(pl.multiple_of(tile * ROWS, ROWS), ROWS)
        cols = pl.ds(pl.multiple_of(half * LANES, LANES), LANES)
        for j in range(1, dir_groups):
            dir_copy(c, j).wait_recv()

        shift = shift_wide[rows, cols]
        turning = turning_ref[rows, cols]
        picks = [shift == k for k in range(-2, 2)]

        def refract(f, sums):
            weight = turning * turn_ref[freq_first + f]
            rest = 1.0 - weight
            moved = [grid_buf[c, d, f] for d in range(dir_total)]

            def shifted(d):
                result = moved[(d - 2) % dir_total]
                for k in (1, 0, -1, -2):
                    result = jnp.where(picks[k + 2], moved[(d - k) % dir_total], result)
                return result

            before = shifted(-1)
            total = jnp.zeros((ROWS, LANES), jnp.float32)
            for d in range(dir_total):
                now = shifted(d)
                turned = rest * now + weight * before
                turned_buf[pl.ds(pl.multiple_of((d * freq_local + f) * ROWS, ROWS), ROWS), :] = turned
                total = total + turned
                before = now
            return sums[0] + total, sums[1] + total * sigma_ref[freq_first + f]

        zero = jnp.zeros((ROWS, LANES), jnp.float32)
        energy, moment = lax.fori_loop(0, freq_local, refract, (zero, zero))
        send_part[pl.ds(0, ROWS), :] = energy
        send_part[pl.ds(ROWS, ROWS), :] = moment

        def swap(n):
            first, last = piece_ends[n]
            first = 0 if n == 0 else (first * freq_local + 2) * ROWS
            piece = pl.ds(first, (last * freq_local + 2) * ROWS - first)
            return pltpu.make_async_remote_copy(
                src_ref=send_part.at[piece],
                dst_ref=recv_part.at[slot, piece],
                send_sem=part_send.at[slot, n],
                recv_sem=part_recv.at[slot, n],
                device_id={"freq": other_freq},
                device_id_type=MESH_ID,
            )

        for n, (first_dir, last_dir) in enumerate(piece_ends):
            size = (last_dir - first_dir) * freq_local
            start = first_dir * freq_local * ROWS
            mine = pl.ds(pl.multiple_of((dir_first + first_dir) * freq_local, 16), size)

            def mix(pair, inner):
                first = turned_buf[pl.ds(2 * pair, depth, stride=ROWS), :]
                second = turned_buf[pl.ds(2 * pair + 1, depth, stride=ROWS), :]
                both = jnp.concatenate([first, second], axis=1)
                high = both.astype(jnp.bfloat16)
                low = (both - high.astype(jnp.float32)).astype(jnp.bfloat16)
                right = jnp.concatenate([high, high, low], axis=0)
                left = jnp.concatenate([matrix[me_freq, mine, :], matrix[other_freq, mine, :]], axis=0)
                part = jnp.dot(left, right, preferred_element_type=jnp.float32)
                for k in range(2):
                    lanes = slice(k * LANES, (k + 1) * LANES)
                    own_part[pl.ds(start + 2 * pair + k, size, stride=ROWS), :] = part[:size, lanes]
                    send_part[pl.ds(start + 2 * ROWS + 2 * pair + k, size, stride=ROWS), :] = part[size:, lanes]
                return inner

            lax.fori_loop(0, ROWS // 2, mix, 0)
            swap(n).start()
        swap(0).wait_recv()

        sea = sea_ref[rows, cols]
        energy = (energy + recv_part[slot, pl.ds(0, ROWS), :]) / bin_total
        moment = (moment + recv_part[slot, pl.ds(ROWS, ROWS), :]) / bin_total
        mean_sigma = moment / (energy + small_eps)
        steepness = energy * mean_sigma * mean_sigma
        white = whitecap_coef * (steepness * steepness)
        nonlinear = sea * (nonlinear_coef * (energy * energy))
        rate = sea * rate_ref[rows, cols]
        cos_w = coswind[rows, cols]
        sin_w = sinwind[rows, cols]
        classes = depth_ref[rows, cols]

        for n, (first_dir, last_dir) in enumerate(piece_ends):
            if n > 0:
                swap(n).wait_recv()

            def source(f, inner):
                sigma = sigma_ref[freq_first + f]
                friction = jnp.full((ROWS, LANES), fric_ref[0, freq_first + f], jnp.float32)
                for k in range(1, class_count):
                    friction = jnp.where(classes == k, fric_ref[k, freq_first + f], friction)
                keep = sea * (1.0 - white * sigma - friction)
                grow = rate * sigma
                for d in range(first_dir, last_dir):
                    spot = d * freq_local + f
                    at = pl.ds(pl.multiple_of(spot * ROWS, ROWS), ROWS)
                    there = pl.ds(pl.multiple_of((spot + 2) * ROWS, ROWS), ROWS)
                    whole = pl.ds(pl.multiple_of(((dir_first + d) * freq_local + f) * ROWS, ROWS), ROWS)
                    align = jnp.maximum(cos_ref[dir_first + d] * cos_w + sin_ref[dir_first + d] * sin_w, 0.0)
                    mixed = own_part[at, :] + recv_part[slot, there, :]
                    out_ref[spot, rows, cols] = turned_buf[whole, :] * (keep + grow * align) + nonlinear * mixed
                return inner

            lax.fori_loop(0, freq_local, source, 0)
        for n in range(len(piece_ends)):
            swap(n).wait_send()
        return carry

    lax.fori_loop(0, chunks, chunk, 0)

    def finish(c, carry):
        for j in range(1, dir_groups):
            dir_copy(c, j).wait_send()
        return carry

    lax.fori_loop(0, chunks, finish, 0)


def shards(
    dir_groups,
    space_groups,
    spectrum,
    land_mask,
    depth_class,
    shift_count,
    turning,
    wind_rate,
    wind_angle,
    cfl,
    freq_turn,
    friction_table,
    transfer,
):
    dir_local, freq_local, row_count, col_count = spectrum.shape
    bins = dir_local * freq_local
    dir_total = dir_local * dir_groups
    freq_total = cfl.shape[0]
    angles = 2.0 * math.pi * np.arange(dir_total) / dir_total
    cosines = jnp.asarray(np.cos(angles), jnp.float32)
    sines = jnp.asarray(np.sin(angles), jnp.float32)
    sigmas = jnp.asarray(0.5 * np.power(1.07, np.arange(freq_total)), jnp.float32)
    chunks = (row_count // ROWS) * (col_count // LANES)
    depth = dir_total * freq_local
    peers = max(dir_groups - 1, 1)
    vmem = pl.BlockSpec(memory_space=pltpu.VMEM)
    smem = pl.BlockSpec(memory_space=pltpu.SMEM)
    anywhere = pl.BlockSpec(memory_space=pl.ANY)
    f32 = jnp.float32
    evolved = pl.pallas_call(
        functools.partial(kernel, dir_groups, space_groups),
        out_shape=pltpu.VMEM((bins, row_count, col_count), f32),
        in_specs=[anywhere] + [vmem] * 6 + [smem] * 6 + [anywhere],
        out_specs=vmem,
        scratch_shapes=[
            pltpu.VMEM((bins * row_count, col_count), f32),
            pltpu.VMEM((chunks, dir_total, freq_local, ROWS, LANES), f32),
            pltpu.VMEM((depth * ROWS, LANES), f32),
            pltpu.VMEM((bins * ROWS, LANES), f32),
            pltpu.VMEM(((bins + 2) * ROWS, LANES), f32),
            pltpu.VMEM((2, (bins + 2) * ROWS, LANES), f32),
            pltpu.VMEM((2, depth, 3 * depth), jnp.bfloat16),
            pltpu.VMEM((dir_total, freq_local, transfer.shape[1]), f32),
            pltpu.VMEM((bins, col_count), f32),
            pltpu.VMEM((bins, col_count), f32),
            pltpu.VMEM((bins, col_count), f32),
            pltpu.VMEM((bins, col_count), f32),
            pltpu.VMEM((row_count, col_count), f32),
            pltpu.VMEM((row_count, col_count), jnp.int32),
            pltpu.VMEM((row_count, col_count), f32),
            pltpu.VMEM((row_count, col_count), f32),
            pltpu.SemaphoreType.DMA((dir_local,)),
            pltpu.SemaphoreType.DMA,
            pltpu.SemaphoreType.DMA((2,)),
            pltpu.SemaphoreType.DMA((2,)),
            pltpu.SemaphoreType.DMA((chunks, peers)),
            pltpu.SemaphoreType.DMA((chunks, peers)),
            pltpu.SemaphoreType.DMA((2, 2)),
            pltpu.SemaphoreType.DMA((2, 2)),
        ],
        compiler_params=pltpu.CompilerParams(
            collective_id=0, has_side_effects=True, vmem_limit_bytes=44 * 1024 * 1024
        ),
        name="wave_step",
    )(
        spectrum.reshape(bins * row_count, col_count),
        land_mask,
        depth_class,
        shift_count.T,
        turning,
        wind_rate,
        wind_angle,
        cfl,
        freq_turn,
        friction_table,
        cosines,
        sines,
        sigmas,
        transfer.reshape(dir_total, freq_total, transfer.shape[1]),
    )
    return evolved.reshape(spectrum.shape)


def solution(mesh):
    points = P(("groups", "space"), None)
    in_specs = (P("dir", "freq", ("groups", "space"), None),) + (points,) * 6 + (P(),) * 4
    return jax.shard_map(
        functools.partial(shards, mesh.shape["dir"], mesh.shape["space"]),
        mesh=mesh,
        in_specs=in_specs,
        out_specs=P("dir", "freq", ("groups", "space"), None),
        check_vma=False,
    )
```

```python
import functools
import math

import jax
import jax.numpy as jnp
import numpy as np
from jax import lax
from jax.experimental import pallas as pl
from jax.experimental.pallas import tpu as pltpu
from jax.sharding import PartitionSpec as P

ROWS = 8
LANES = 128
MESH_ID = pl.DeviceIdType.MESH

whitecap_coef = 0.01
nonlinear_coef = 0.5
small_eps = 1e-05


def kernel(
    dir_groups,
    space_groups,
    spectrum_ref,
    land_hbm,
    depth_hbm,
    shift_hbm,
    turning_hbm,
    rate_hbm,
    wind_hbm,
    cfl_hbm,
    turn_hbm,
    fric_hbm,
    cos_hbm,
    sin_hbm,
    sigma_hbm,
    transfer_ref,
    out_ref,
    land_ref,
    depth_ref,
    shift_ref,
    turning_ref,
    rate_ref,
    wind_ref,
    cfl_ref,
    turn_ref,
    fric_ref,
    cos_ref,
    sin_ref,
    sigma_ref,
    small_sem,
    spec_ref,
    grid_buf,
    turned_buf,
    own_part,
    send_part,
    recv_part,
    matrix,
    raw_matrix,
    edge_top,
    edge_bot,
    halo_up,
    halo_dn,
    sea_ref,
    shift_wide,
    coswind,
    sinwind,
    spec_sem,
    matrix_sem,
    halo_send,
    halo_recv,
    dir_send,
    dir_recv,
    part_send,
    part_recv,
):
    me_dir = lax.axis_index("dir")
    me_space = lax.axis_index("space")
    me_freq = lax.axis_index("freq")
    other_freq = 1 - me_freq
    dir_total, freq_local = grid_buf.shape[1], grid_buf.shape[2]
    dir_local = dir_total // dir_groups
    bins = dir_local * freq_local
    row_count = out_ref.shape[1]
    col_count = out_ref.shape[2]
    tiles = row_count // ROWS
    halves = col_count // LANES
    chunks = tiles * halves
    class_count = fric_ref.shape[0]
    bin_total = transfer_ref.shape[2]
    dir_first = me_dir * dir_local
    freq_first = pl.multiple_of(me_freq * freq_local, 8)

    barrier = pltpu.get_barrier_semaphore()
    for j in range(1, dir_groups):
        pl.semaphore_signal(
            barrier, inc=1, device_id={"dir": lax.rem(me_dir + j, dir_groups)}, device_id_type=MESH_ID
        )
    pl.semaphore_signal(barrier, inc=1, device_id={"freq": other_freq}, device_id_type=MESH_ID)

    @pl.when(me_space > 0)
    def _():
        pl.semaphore_signal(barrier, inc=1, device_id={"space": me_space - 1}, device_id_type=MESH_ID)

    @pl.when(me_space < space_groups - 1)
    def _():
        pl.semaphore_signal(barrier, inc=1, device_id={"space": me_space + 1}, device_id_type=MESH_ID)

    small = [
        pltpu.make_async_copy(source, table, small_sem.at[n])
        for n, (source, table) in enumerate(
            (
                (land_hbm, land_ref),
                (cfl_hbm, cfl_ref),
                (cos_hbm, cos_ref),
                (sin_hbm, sin_ref),
                (turning_hbm, turning_ref),
                (turn_hbm, turn_ref),
                (fric_hbm, fric_ref),
                (sigma_hbm, sigma_ref),
                (depth_hbm, depth_ref),
                (shift_hbm, shift_ref),
                (rate_hbm, rate_ref),
                (wind_hbm, wind_ref),
            )
        )
    ]
    for copy in small:
        copy.start()

    def spec_copy(d):
        piece = pl.ds(pl.multiple_of(d * freq_local * row_count, ROWS), freq_local * row_count)
        return pltpu.make_async_copy(spectrum_ref.at[piece], spec_ref.at[piece], spec_sem.at[d])

    def start_copy(d, carry):
        spec_copy(d).start()
        return carry

    lax.fori_loop(0, dir_local, start_copy, 0)
    matrix_copy = pltpu.make_async_copy(
        transfer_ref.at[:, pl.ds(freq_first, freq_local), :], raw_matrix, matrix_sem
    )
    matrix_copy.start()

    for copy in small[:4]:
        copy.wait()
    sea_ref[...] = jnp.where(land_ref[...] == 1, 1.0, 0.0)

    first_sea = sea_ref[pl.ds(0, ROWS), :]
    last_sea = sea_ref[pl.ds(row_count - ROWS, ROWS), :]

    def pack(b):
        base = pl.multiple_of(b * row_count, ROWS)
        top = spec_ref[pl.ds(base, ROWS), :] * first_sea
        low = spec_ref[pl.ds(base + row_count - ROWS, ROWS), :] * last_sea
        edge_top[pl.ds(b, 1), :] = top[:1]
        edge_bot[pl.ds(b, 1), :] = low[ROWS - 1 :]

    pl.semaphore_wait(
        barrier,
        dir_groups
        + (me_space > 0).astype(jnp.int32)
        + (me_space < space_groups - 1).astype(jnp.int32),
    )

    up_copy = pltpu.make_async_remote_copy(
        src_ref=edge_top,
        dst_ref=halo_dn,
        send_sem=halo_send.at[0],
        recv_sem=halo_recv.at[0],
        device_id={"space": jnp.maximum(me_space - 1, 0)},
        device_id_type=MESH_ID,
    )
    down_copy = pltpu.make_async_remote_copy(
        src_ref=edge_bot,
        dst_ref=halo_up,
        send_sem=halo_send.at[1],
        recv_sem=halo_recv.at[1],
        device_id={"space": jnp.minimum(me_space + 1, space_groups - 1)},
        device_id_type=MESH_ID,
    )

    def dir_copy(c, j, first=0, count=dir_local):
        region = grid_buf.at[c, pl.ds(dir_first + first, count)]
        return pltpu.make_async_remote_copy(
            src_ref=region,
            dst_ref=region,
            send_sem=dir_send.at[c, j - 1],
            recv_sem=dir_recv.at[c, j - 1],
            device_id={"dir": lax.rem(me_dir + j, dir_groups)},
            device_id_type=MESH_ID,
        )

    row_id = lax.broadcasted_iota(jnp.int32, (ROWS, col_count), 0)
    col_id = lax.broadcasted_iota(jnp.int32, (ROWS, col_count), 1)

    def propagate(tile, place):
        sea = sea_ref[pl.ds(tile * ROWS, ROWS), :]
        if tile > 0:
            sea_prev = sea_ref[pl.ds(tile * ROWS - ROWS, ROWS), :]
        if tile < tiles - 1:
            sea_next = sea_ref[pl.ds(tile * ROWS + ROWS, ROWS), :]

        def per_dir(d, carry):
            if place == 0:
                spec_copy(d).wait()
            cos_d = cos_ref[dir_first + d]
            sin_d = sin_ref[dir_first + d]

            def per_freq(f, inner):
                b = d * freq_local + f
                if place == 0:
                    pack(b)
                base = pl.multiple_of(b * row_count, ROWS)
                here = spec_ref[pl.ds(base + tile * ROWS, ROWS), :] * sea
                if tile > 0:
                    prev = spec_ref[pl.ds(base + (tile - 1) * ROWS, ROWS), :] * sea_prev
                    above = pltpu.roll(jnp.where(row_id == ROWS - 1, prev, here), 1, 0)
                else:
                    above = jnp.where(row_id == 0, halo_up[pl.ds(b, 1), :], pltpu.roll(here, 1, 0))
                if tile < tiles - 1:
                    later = spec_ref[pl.ds(base + (tile + 1) * ROWS, ROWS), :] * sea_next
                    below = pltpu.roll(jnp.where(row_id == 0, later, here), ROWS - 1, 0)
                else:
                    below = jnp.where(
                        row_id == ROWS - 1, halo_dn[pl.ds(b, 1), :], pltpu.roll(here, ROWS - 1, 0)
                    )
                left = jnp.where(col_id == 0, 0.0, pltpu.roll(here, 1, 1))
                right = jnp.where(col_id == col_count - 1, 0.0, pltpu.roll(here, col_count - 1, 1))
                speed = cfl_ref[freq_first + f]
                speed_x = speed * cos_d
                speed_y = speed * sin_d
                moved = here - jnp.maximum(speed_x, 0.0) * (here - above)
                moved = moved - jnp.minimum(speed_x, 0.0) * (below - here)
                moved = moved - jnp.maximum(speed_y, 0.0) * (here - left)
                moved = moved - jnp.minimum(speed_y, 0.0) * (right - here)
                moved = moved * sea
                for h in range(halves):
                    grid_buf[place * halves + h, dir_first + d, f] = moved[:, h * LANES : (h + 1) * LANES]
                return inner

            lax.fori_loop(0, freq_local, per_freq, 0, unroll=4)
            if place == 0:
                for h in range(halves):
                    for j in range(1, dir_groups):
                        dir_copy(h, j, d, 1).start()
            return carry

        lax.fori_loop(0, dir_local, per_dir, 0)
        if place > 0:
            for h in range(halves):
                for j in range(1, dir_groups):
                    dir_copy(place * halves + h, j).start()

    for place in range(tiles - 2):
        propagate(place + 1, place)

    @pl.when(me_space > 0)
    def _():
        up_copy.start()

    @pl.when(me_space < space_groups - 1)
    def _():
        down_copy.start()

    @pl.when(me_space > 0)
    def _():
        up_copy.wait_send()
        down_copy.wait_recv()

    @pl.when(me_space == 0)
    def _():
        halo_up[...] = jnp.zeros_like(halo_up)

    @pl.when(me_space < space_groups - 1)
    def _():
        down_copy.wait_send()
        up_copy.wait_recv()

    @pl.when(me_space == space_groups - 1)
    def _():
        halo_dn[...] = jnp.zeros_like(halo_dn)

    propagate(0, tiles - 2)
    propagate(tiles - 1, tiles - 1)

    for copy in small[4:]:
        copy.wait()
    coswind[...] = jnp.cos(wind_ref[...])
    sinwind[...] = jnp.sin(wind_ref[...])
    shift_tiles = shift_ref.shape[0]
    width = col_count // shift_tiles
    tile_of = lax.broadcasted_iota(jnp.int32, (shift_tiles, col_count), 1) // width
    tile_id = lax.broadcasted_iota(jnp.int32, (shift_tiles, col_count), 0)
    shift_wide[...] = lax.dot_general(
        shift_ref[...].astype(jnp.float32),
        (tile_of == tile_id).astype(jnp.float32),
        (((0,), (0,)), ((), ())),
        preferred_element_type=jnp.float32,
    ).astype(jnp.int32)

    matrix_copy.wait()
    depth = dir_total * freq_local
    for m in range(bin_total // LANES):
        block = raw_matrix[:, :, m * LANES : (m + 1) * LANES].reshape(depth, LANES)
        high = block.astype(jnp.bfloat16).astype(jnp.float32)
        low = block - high
        turned_block = jnp.concatenate([high, low, high], axis=0).T.astype(jnp.bfloat16)
        for piece in range(LANES // freq_local):
            d, g = divmod(m * (LANES // freq_local) + piece, 2)
            matrix[g, pl.ds(d * freq_local, freq_local), :] = turned_block[
                piece * freq_local : (piece + 1) * freq_local
            ]

    middle = (dir_local + 1) // 2
    piece_ends = ((0, middle), (middle, dir_local))

    def chunk(c, carry):
        slot = c % 2
        place = c // halves
        half = c % halves
        tile = jnp.where(place < tiles - 2, place + 1, jnp.where(place == tiles - 2, 0, tiles - 1))
        rows = pl.ds(pl.multiple_of(tile * ROWS, ROWS), ROWS)
        cols = pl.ds(pl.multiple_of(half * LANES, LANES), LANES)
        for j in range(1, dir_groups):
            dir_copy(c, j).wait_recv()

        shift = shift_wide[rows, cols]
        turning = turning_ref[rows, cols]
        picks = [shift == k for k in range(-2, 2)]

        def refract(f, sums):
            weight = turning * turn_ref[freq_first + f]
            rest = 1.0 - weight
            moved = [grid_buf[c, d, f] for d in range(dir_total)]

            def shifted(d):
                result = moved[(d - 2) % dir_total]
                for k in (1, 0, -1, -2):
                    result = jnp.where(picks[k + 2], moved[(d - k) % dir_total], result)
                return result

            before = shifted(-1)
            total = jnp.zeros((ROWS, LANES), jnp.float32)
            for d in range(dir_total):
                now = shifted(d)
                turned = rest * now + weight * before
                turned_buf[pl.ds(pl.multiple_of((d * freq_local + f) * ROWS, ROWS), ROWS), :] = turned
                total = total + turned
                before = now
            return sums[0] + total, sums[1] + total * sigma_ref[freq_first + f]

        zero = jnp.zeros((ROWS, LANES), jnp.float32)
        energy, moment = lax.fori_loop(0, freq_local, refract, (zero, zero))
        send_part[pl.ds(0, ROWS), :] = energy
        send_part[pl.ds(ROWS, ROWS), :] = moment

        def swap(n):
            first, last = piece_ends[n]
            first = 0 if n == 0 else (first * freq_local + 2) * ROWS
            piece = pl.ds(first, (last * freq_local + 2) * ROWS - first)
            return pltpu.make_async_remote_copy(
                src_ref=send_part.at[piece],
                dst_ref=recv_part.at[slot, piece],
                send_sem=part_send.at[slot, n],
                recv_sem=part_recv.at[slot, n],
                device_id={"freq": other_freq},
                device_id_type=MESH_ID,
            )

        for n, (first_dir, last_dir) in enumerate(piece_ends):
            size = (last_dir - first_dir) * freq_local
            start = first_dir * freq_local * ROWS
            mine = pl.ds(pl.multiple_of((dir_first + first_dir) * freq_local, 16), size)

            def mix(pair, inner):
                first = turned_buf[pl.ds(2 * pair, depth, stride=ROWS), :]
                second = turned_buf[pl.ds(2 * pair + 1, depth, stride=ROWS), :]
                both = jnp.concatenate([first, second], axis=1)
                high = both.astype(jnp.bfloat16)
                low = (both - high.astype(jnp.float32)).astype(jnp.bfloat16)
                right = jnp.concatenate([high, high, low], axis=0)
                left = jnp.concatenate([matrix[me_freq, mine, :], matrix[other_freq, mine, :]], axis=0)
                part = jnp.dot(left, right, preferred_element_type=jnp.float32)
                for k in range(2):
                    lanes = slice(k * LANES, (k + 1) * LANES)
                    own_part[pl.ds(start + 2 * pair + k, size, stride=ROWS), :] = part[:size, lanes]
                    send_part[pl.ds(start + 2 * ROWS + 2 * pair + k, size, stride=ROWS), :] = part[size:, lanes]
                return inner

            lax.fori_loop(0, ROWS // 2, mix, 0)
            swap(n).start()
        swap(0).wait_recv()

        sea = sea_ref[rows, cols]
        energy = (energy + recv_part[slot, pl.ds(0, ROWS), :]) / bin_total
        moment = (moment + recv_part[slot, pl.ds(ROWS, ROWS), :]) / bin_total
        mean_sigma = moment / (energy + small_eps)
        steepness = energy * mean_sigma * mean_sigma
        white = whitecap_coef * (steepness * steepness)
        nonlinear = sea * (nonlinear_coef * (energy * energy))
        rate = sea * rate_ref[rows, cols]
        cos_w = coswind[rows, cols]
        sin_w = sinwind[rows, cols]
        classes = depth_ref[rows, cols]

        for n, (first_dir, last_dir) in enumerate(piece_ends):
            if n > 0:
                swap(n).wait_recv()

            def source(f, inner):
                sigma = sigma_ref[freq_first + f]
                friction = jnp.full((ROWS, LANES), fric_ref[0, freq_first + f], jnp.float32)
                for k in range(1, class_count):
                    friction = jnp.where(classes == k, fric_ref[k, freq_first + f], friction)
                keep = sea * (1.0 - white * sigma - friction)
                grow = rate * sigma
                for d in range(first_dir, last_dir):
                    spot = d * freq_local + f
                    at = pl.ds(pl.multiple_of(spot * ROWS, ROWS), ROWS)
                    there = pl.ds(pl.multiple_of((spot + 2) * ROWS, ROWS), ROWS)
                    whole = pl.ds(pl.multiple_of(((dir_first + d) * freq_local + f) * ROWS, ROWS), ROWS)
                    align = jnp.maximum(cos_ref[dir_first + d] * cos_w + sin_ref[dir_first + d] * sin_w, 0.0)
                    mixed = own_part[at, :] + recv_part[slot, there, :]
                    out_ref[spot, rows, cols] = turned_buf[whole, :] * (keep + grow * align) + nonlinear * mixed
                return inner

            lax.fori_loop(0, freq_local, source, 0)
        for n in range(len(piece_ends)):
            swap(n).wait_send()
        return carry

    lax.fori_loop(0, chunks, chunk, 0)

    def finish(c, carry):
        for j in range(1, dir_groups):
            dir_copy(c, j).wait_send()
        return carry

    lax.fori_loop(0, chunks, finish, 0)


def shards(
    dir_groups,
    space_groups,
    spectrum,
    land_mask,
    depth_class,
    shift_count,
    turning,
    wind_rate,
    wind_angle,
    cfl,
    freq_turn,
    friction_table,
    transfer,
):
    dir_local, freq_local, row_count, col_count = spectrum.shape
    bins = dir_local * freq_local
    dir_total = dir_local * dir_groups
    freq_total = cfl.shape[0]
    angles = 2.0 * math.pi * np.arange(dir_total) / dir_total
    cosines = jnp.asarray(np.cos(angles), jnp.float32)
    sines = jnp.asarray(np.sin(angles), jnp.float32)
    sigmas = jnp.asarray(0.5 * np.power(1.07, np.arange(freq_total)), jnp.float32)
    chunks = (row_count // ROWS) * (col_count // LANES)
    depth = dir_total * freq_local
    peers = max(dir_groups - 1, 1)
    vmem = pl.BlockSpec(memory_space=pltpu.VMEM)
    hbm = pl.BlockSpec(memory_space=pltpu.HBM)
    shift_tiles = shift_count.shape[1]
    class_count = friction_table.shape[0]
    points = (row_count, col_count)
    f32 = jnp.float32
    evolved = pl.pallas_call(
        functools.partial(kernel, dir_groups, space_groups),
        out_shape=pltpu.VMEM((bins, row_count, col_count), f32),
        in_specs=[hbm] * 14,
        out_specs=vmem,
        scratch_shapes=[
            pltpu.VMEM(points, jnp.int32),
            pltpu.VMEM(points, jnp.int32),
            pltpu.VMEM((shift_tiles, row_count), jnp.int32),
            pltpu.VMEM(points, f32),
            pltpu.VMEM(points, f32),
            pltpu.VMEM(points, f32),
            pltpu.SMEM((freq_total,), f32),
            pltpu.SMEM((freq_total,), f32),
            pltpu.SMEM((class_count, freq_total), f32),
            pltpu.SMEM((dir_total,), f32),
            pltpu.SMEM((dir_total,), f32),
            pltpu.SMEM((freq_total,), f32),
            pltpu.SemaphoreType.DMA((12,)),
            pltpu.VMEM((bins * row_count, col_count), f32),
            pltpu.VMEM((chunks, dir_total, freq_local, ROWS, LANES), f32),
            pltpu.VMEM((depth * ROWS, LANES), f32),
            pltpu.VMEM((bins * ROWS, LANES), f32),
            pltpu.VMEM(((bins + 2) * ROWS, LANES), f32),
            pltpu.VMEM((2, (bins + 2) * ROWS, LANES), f32),
            pltpu.VMEM((2, depth, 3 * depth), jnp.bfloat16),
            pltpu.VMEM((dir_total, freq_local, transfer.shape[1]), f32),
            pltpu.VMEM((bins, col_count), f32),
            pltpu.VMEM((bins, col_count), f32),
            pltpu.VMEM((bins, col_count), f32),
            pltpu.VMEM((bins, col_count), f32),
            pltpu.VMEM((row_count, col_count), f32),
            pltpu.VMEM((row_count, col_count), jnp.int32),
            pltpu.VMEM((row_count, col_count), f32),
            pltpu.VMEM((row_count, col_count), f32),
            pltpu.SemaphoreType.DMA((dir_local,)),
            pltpu.SemaphoreType.DMA,
            pltpu.SemaphoreType.DMA((2,)),
            pltpu.SemaphoreType.DMA((2,)),
            pltpu.SemaphoreType.DMA((chunks, peers)),
            pltpu.SemaphoreType.DMA((chunks, peers)),
            pltpu.SemaphoreType.DMA((2, 2)),
            pltpu.SemaphoreType.DMA((2, 2)),
        ],
        compiler_params=pltpu.CompilerParams(
            collective_id=0, has_side_effects=True, vmem_limit_bytes=52 * 1024 * 1024
        ),
        name="wave_step",
    )(
        spectrum.reshape(bins * row_count, col_count),
        land_mask,
        depth_class,
        shift_count.T,
        turning,
        wind_rate,
        wind_angle,
        cfl,
        freq_turn,
        friction_table,
        cosines,
        sines,
        sigmas,
        transfer.reshape(dir_total, freq_total, transfer.shape[1]),
    )
    return evolved.reshape(spectrum.shape)


def solution(mesh):
    points = P(("groups", "space"), None)
    in_specs = (P("dir", "freq", ("groups", "space"), None),) + (points,) * 6 + (P(),) * 4
    return jax.shard_map(
        functools.partial(shards, mesh.shape["dir"], mesh.shape["space"]),
        mesh=mesh,
        in_specs=in_specs,
        out_specs=P("dir", "freq", ("groups", "space"), None),
        check_vma=False,
    )
```

```python
import functools
import math

import jax
import jax.numpy as jnp
import numpy as np
from jax import lax
from jax.experimental import pallas as pl
from jax.experimental.pallas import tpu as pltpu
from jax.sharding import PartitionSpec as P

ROWS = 8
LANES = 128
TAIL = 4
MESH_ID = pl.DeviceIdType.MESH

whitecap_coef = 0.01
nonlinear_coef = 0.5
small_eps = 1e-05


def kernel(
    dir_groups,
    space_groups,
    spectrum_ref,
    land_hbm,
    depth_hbm,
    shift_hbm,
    turning_hbm,
    rate_hbm,
    wind_hbm,
    cfl_hbm,
    turn_hbm,
    fric_hbm,
    cos_hbm,
    sin_hbm,
    sigma_hbm,
    transfer_ref,
    out_ref,
    land_ref,
    depth_ref,
    shift_ref,
    turning_ref,
    rate_ref,
    wind_ref,
    cfl_ref,
    turn_ref,
    fric_ref,
    cos_ref,
    sin_ref,
    sigma_ref,
    small_sem,
    spec_ref,
    grid_buf,
    turned_buf,
    own_part,
    send_part,
    recv_part,
    matrix,
    raw_matrix,
    raw_other,
    tail_matrix,
    tail_send,
    tail_recv,
    edge_top,
    edge_bot,
    halo_up,
    halo_dn,
    sea_ref,
    shift_wide,
    coswind,
    sinwind,
    spec_sem,
    matrix_sem,
    other_sem,
    tail_send_sem,
    tail_recv_sem,
    halo_send,
    halo_recv,
    dir_send,
    dir_recv,
    part_send,
    part_recv,
):
    me_dir = lax.axis_index("dir")
    me_space = lax.axis_index("space")
    me_freq = lax.axis_index("freq")
    other_freq = 1 - me_freq
    dir_total, freq_local = grid_buf.shape[1], grid_buf.shape[2]
    dir_local = dir_total // dir_groups
    bins = dir_local * freq_local
    row_count = out_ref.shape[1]
    col_count = out_ref.shape[2]
    tiles = row_count // ROWS
    halves = col_count // LANES
    chunks = tiles * halves
    class_count = fric_ref.shape[0]
    bin_total = transfer_ref.shape[2]
    dir_first = me_dir * dir_local
    freq_first = pl.multiple_of(me_freq * freq_local, 8)

    barrier = pltpu.get_barrier_semaphore()
    for j in range(1, dir_groups):
        pl.semaphore_signal(
            barrier, inc=1, device_id={"dir": lax.rem(me_dir + j, dir_groups)}, device_id_type=MESH_ID
        )
    pl.semaphore_signal(barrier, inc=1, device_id={"freq": other_freq}, device_id_type=MESH_ID)

    @pl.when(me_space > 0)
    def _():
        pl.semaphore_signal(barrier, inc=1, device_id={"space": me_space - 1}, device_id_type=MESH_ID)

    @pl.when(me_space < space_groups - 1)
    def _():
        pl.semaphore_signal(barrier, inc=1, device_id={"space": me_space + 1}, device_id_type=MESH_ID)

    small = [
        pltpu.make_async_copy(source, table, small_sem.at[n])
        for n, (source, table) in enumerate(
            (
                (land_hbm, land_ref),
                (cfl_hbm, cfl_ref),
                (cos_hbm, cos_ref),
                (sin_hbm, sin_ref),
                (turning_hbm, turning_ref),
                (turn_hbm, turn_ref),
                (fric_hbm, fric_ref),
                (sigma_hbm, sigma_ref),
                (depth_hbm, depth_ref),
                (shift_hbm, shift_ref),
                (rate_hbm, rate_ref),
                (wind_hbm, wind_ref),
            )
        )
    ]
    for copy in small:
        copy.start()

    def spec_copy(d):
        piece = pl.ds(pl.multiple_of(d * freq_local * row_count, ROWS), freq_local * row_count)
        return pltpu.make_async_copy(spectrum_ref.at[piece], spec_ref.at[piece], spec_sem.at[d])

    def start_copy(d, carry):
        spec_copy(d).start()
        return carry

    lax.fori_loop(0, dir_local, start_copy, 0)
    matrix_copy = pltpu.make_async_copy(
        transfer_ref.at[:, pl.ds(freq_first, freq_local), :], raw_matrix, matrix_sem
    )
    matrix_copy.start()
    other_copy = pltpu.make_async_copy(
        transfer_ref.at[:, pl.ds(pl.multiple_of(other_freq * freq_local + freq_local - ROWS, ROWS), ROWS), :],
        raw_other,
        other_sem,
    )
    other_copy.start()

    for copy in small[:4]:
        copy.wait()
    sea_ref[...] = jnp.where(land_ref[...] == 1, 1.0, 0.0)

    first_sea = sea_ref[pl.ds(0, ROWS), :]
    last_sea = sea_ref[pl.ds(row_count - ROWS, ROWS), :]

    def pack(b):
        base = pl.multiple_of(b * row_count, ROWS)
        top = spec_ref[pl.ds(base, ROWS), :] * first_sea
        low = spec_ref[pl.ds(base + row_count - ROWS, ROWS), :] * last_sea
        edge_top[pl.ds(b, 1), :] = top[:1]
        edge_bot[pl.ds(b, 1), :] = low[ROWS - 1 :]

    pl.semaphore_wait(
        barrier,
        dir_groups
        + (me_space > 0).astype(jnp.int32)
        + (me_space < space_groups - 1).astype(jnp.int32),
    )

    up_copy = pltpu.make_async_remote_copy(
        src_ref=edge_top,
        dst_ref=halo_dn,
        send_sem=halo_send.at[0],
        recv_sem=halo_recv.at[0],
        device_id={"space": jnp.maximum(me_space - 1, 0)},
        device_id_type=MESH_ID,
    )
    down_copy = pltpu.make_async_remote_copy(
        src_ref=edge_bot,
        dst_ref=halo_up,
        send_sem=halo_send.at[1],
        recv_sem=halo_recv.at[1],
        device_id={"space": jnp.minimum(me_space + 1, space_groups - 1)},
        device_id_type=MESH_ID,
    )

    head = freq_local - TAIL

    def dir_copy(c, j, first=0, count=dir_local, low=0, bands=freq_local, sem=None):
        sem = c if sem is None else sem
        region = grid_buf.at[c, pl.ds(dir_first + first, count), pl.ds(low, bands)]
        return pltpu.make_async_remote_copy(
            src_ref=region,
            dst_ref=region,
            send_sem=dir_send.at[sem, j - 1],
            recv_sem=dir_recv.at[sem, j - 1],
            device_id={"dir": lax.rem(me_dir + j, dir_groups)},
            device_id_type=MESH_ID,
        )

    def last_copy(j, n):
        if n == 0:
            return dir_copy(chunks - 1, j, low=0, bands=head)
        return dir_copy(chunks - 1, j, low=head, bands=TAIL, sem=chunks)

    row_id = lax.broadcasted_iota(jnp.int32, (ROWS, col_count), 0)
    col_id = lax.broadcasted_iota(jnp.int32, (ROWS, col_count), 1)

    def propagate(tile, place):
        sea = sea_ref[pl.ds(tile * ROWS, ROWS), :]
        if tile > 0:
            sea_prev = sea_ref[pl.ds(tile * ROWS - ROWS, ROWS), :]
        if tile < tiles - 1:
            sea_next = sea_ref[pl.ds(tile * ROWS + ROWS, ROWS), :]

        def per_dir(d, carry):
            if place == 0:
                spec_copy(d).wait()
            cos_d = cos_ref[dir_first + d]
            sin_d = sin_ref[dir_first + d]

            def per_freq(f, inner):
                b = d * freq_local + f
                if place == 0:
                    pack(b)
                base = pl.multiple_of(b * row_count, ROWS)
                here = spec_ref[pl.ds(base + tile * ROWS, ROWS), :] * sea
                if tile > 0:
                    prev = spec_ref[pl.ds(base + (tile - 1) * ROWS, ROWS), :] * sea_prev
                    above = pltpu.roll(jnp.where(row_id == ROWS - 1, prev, here), 1, 0)
                else:
                    above = jnp.where(row_id == 0, halo_up[pl.ds(b, 1), :], pltpu.roll(here, 1, 0))
                if tile < tiles - 1:
                    later = spec_ref[pl.ds(base + (tile + 1) * ROWS, ROWS), :] * sea_next
                    below = pltpu.roll(jnp.where(row_id == 0, later, here), ROWS - 1, 0)
                else:
                    below = jnp.where(
                        row_id == ROWS - 1, halo_dn[pl.ds(b, 1), :], pltpu.roll(here, ROWS - 1, 0)
                    )
                left = jnp.where(col_id == 0, 0.0, pltpu.roll(here, 1, 1))
                right = jnp.where(col_id == col_count - 1, 0.0, pltpu.roll(here, col_count - 1, 1))
                speed = cfl_ref[freq_first + f]
                speed_x = speed * cos_d
                speed_y = speed * sin_d
                moved = here - jnp.maximum(speed_x, 0.0) * (here - above)
                moved = moved - jnp.minimum(speed_x, 0.0) * (below - here)
                moved = moved - jnp.maximum(speed_y, 0.0) * (here - left)
                moved = moved - jnp.minimum(speed_y, 0.0) * (right - here)
                moved = moved * sea
                for h in range(halves):
                    grid_buf[place * halves + h, dir_first + d, f] = moved[:, h * LANES : (h + 1) * LANES]
                return inner

            lax.fori_loop(0, freq_local, per_freq, 0, unroll=4)
            if place == 0:
                for h in range(halves):
                    for j in range(1, dir_groups):
                        dir_copy(h, j, d, 1).start()
            return carry

        lax.fori_loop(0, dir_local, per_dir, 0)
        if place > 0:
            for h in range(halves):
                for j in range(1, dir_groups):
                    if place * halves + h == chunks - 1:
                        for n in range(2):
                            last_copy(j, n).start()
                    else:
                        dir_copy(place * halves + h, j).start()

    for place in range(tiles - 2):
        propagate(place + 1, place)

    @pl.when(me_space > 0)
    def _():
        up_copy.start()

    @pl.when(me_space < space_groups - 1)
    def _():
        down_copy.start()

    @pl.when(me_space > 0)
    def _():
        up_copy.wait_send()
        down_copy.wait_recv()

    @pl.when(me_space == 0)
    def _():
        halo_up[...] = jnp.zeros_like(halo_up)

    @pl.when(me_space < space_groups - 1)
    def _():
        down_copy.wait_send()
        up_copy.wait_recv()

    @pl.when(me_space == space_groups - 1)
    def _():
        halo_dn[...] = jnp.zeros_like(halo_dn)

    propagate(0, tiles - 2)
    propagate(tiles - 1, tiles - 1)

    for copy in small[4:]:
        copy.wait()
    coswind[...] = jnp.cos(wind_ref[...])
    sinwind[...] = jnp.sin(wind_ref[...])
    shift_tiles = shift_ref.shape[0]
    width = col_count // shift_tiles
    tile_of = lax.broadcasted_iota(jnp.int32, (shift_tiles, col_count), 1) // width
    tile_id = lax.broadcasted_iota(jnp.int32, (shift_tiles, col_count), 0)
    shift_wide[...] = lax.dot_general(
        shift_ref[...].astype(jnp.float32),
        (tile_of == tile_id).astype(jnp.float32),
        (((0,), (0,)), ((), ())),
        preferred_element_type=jnp.float32,
    ).astype(jnp.int32)

    matrix_copy.wait()
    other_copy.wait()
    depth = dir_total * freq_local
    for m in range(bin_total // LANES):
        block = raw_matrix[:, :, m * LANES : (m + 1) * LANES].reshape(depth, LANES)
        high = block.astype(jnp.bfloat16).astype(jnp.float32)
        low = block - high
        turned_block = jnp.concatenate([high, low, high], axis=0).T.astype(jnp.bfloat16)
        for piece in range(LANES // freq_local):
            d, g = divmod(m * (LANES // freq_local) + piece, 2)
            matrix[g, pl.ds(d * freq_local, freq_local), :] = turned_block[
                piece * freq_local : (piece + 1) * freq_local
            ]

    middle = (dir_local + 1) // 2
    piece_ends = ((0, middle), (middle, dir_local))

    eight = lax.broadcasted_iota(jnp.int32, (dir_total // 2, ROWS, LANES), 1)
    for m in range(bin_total // LANES):
        lanes = slice(m * LANES, (m + 1) * LANES)
        for side in range(2):
            block = raw_other[:, :, lanes] if side else raw_matrix[:, freq_local - ROWS :, lanes]
            pairs = block.reshape(dir_total // 2, 2, ROWS, LANES)
            block = jnp.where(eight < TAIL, pltpu.roll(pairs[:, 0], TAIL, 1), pairs[:, 1])
            block = block.reshape(dir_total * TAIL, LANES)
            high = block.astype(jnp.bfloat16).astype(jnp.float32)
            low = block - high
            turned_block = jnp.concatenate([high, low, high], axis=0).T.astype(jnp.bfloat16)
            for piece in range(LANES // freq_local):
                d, g = divmod(m * (LANES // freq_local) + piece, 2)
                tail_matrix[side, g, pl.ds(d * freq_local, freq_local), :] = turned_block[
                    piece * freq_local : (piece + 1) * freq_local
                ]

    def chunk(c, last):
        slot = c % 2
        if last:
            tile, half = tiles - 1, halves - 1
        else:
            place = c // halves
            half = c % halves
            tile = jnp.where(place < tiles - 2, place + 1, jnp.where(place == tiles - 2, 0, tiles - 1))
        rows = pl.ds(tile * ROWS if last else pl.multiple_of(tile * ROWS, ROWS), ROWS)
        cols = pl.ds(half * LANES if last else pl.multiple_of(half * LANES, LANES), LANES)
        for j in range(1, dir_groups):
            copy = last_copy(j, 0) if last else dir_copy(c, j)
            copy.wait_recv()

        shift = shift_wide[rows, cols]
        turning = turning_ref[rows, cols]
        picks = [shift == k for k in range(-2, 2)]

        def refract(in_tail, f, sums):
            weight = turning * turn_ref[freq_first + f]
            rest = 1.0 - weight
            moved = [grid_buf[c, d, f] for d in range(dir_total)]

            def shifted(d):
                result = moved[(d - 2) % dir_total]
                for k in (1, 0, -1, -2):
                    result = jnp.where(picks[k + 2], moved[(d - k) % dir_total], result)
                return result

            before = shifted(-1)
            total = jnp.zeros((ROWS, LANES), jnp.float32)
            for d in range(dir_total):
                now = shifted(d)
                turned = rest * now + weight * before
                turned_buf[pl.ds(pl.multiple_of((d * freq_local + f) * ROWS, ROWS), ROWS), :] = turned
                if in_tail:
                    spot = (d * TAIL + f - head + 2) * ROWS
                    tail_send[pl.ds(pl.multiple_of(spot, ROWS), ROWS), :] = turned
                total = total + turned
                before = now
            return sums[0] + total, sums[1] + total * sigma_ref[freq_first + f]

        zero = jnp.zeros((ROWS, LANES), jnp.float32)
        energy, moment = lax.fori_loop(
            0, head if last else freq_local, functools.partial(refract, False), (zero, zero)
        )
        if last:

            def clear(d, inner):
                spot = pl.multiple_of((d * freq_local + head) * ROWS, ROWS)
                turned_buf[pl.ds(spot, TAIL * ROWS), :] = jnp.zeros((TAIL * ROWS, LANES), jnp.float32)
                return inner

            lax.fori_loop(0, dir_total, clear, 0)
        send_part[pl.ds(0, ROWS), :] = energy
        send_part[pl.ds(ROWS, ROWS), :] = moment

        def swap(n):
            first, last = piece_ends[n]
            first = 0 if n == 0 else (first * freq_local + 2) * ROWS
            piece = pl.ds(first, (last * freq_local + 2) * ROWS - first)
            return pltpu.make_async_remote_copy(
                src_ref=send_part.at[piece],
                dst_ref=recv_part.at[slot, piece],
                send_sem=part_send.at[slot, n],
                recv_sem=part_recv.at[slot, n],
                device_id={"freq": other_freq},
                device_id_type=MESH_ID,
            )

        for n, (first_dir, last_dir) in enumerate(piece_ends):
            size = (last_dir - first_dir) * freq_local
            start = first_dir * freq_local * ROWS
            mine = pl.ds(pl.multiple_of((dir_first + first_dir) * freq_local, 16), size)

            def mix(pair, inner):
                first = turned_buf[pl.ds(2 * pair, depth, stride=ROWS), :]
                second = turned_buf[pl.ds(2 * pair + 1, depth, stride=ROWS), :]
                both = jnp.concatenate([first, second], axis=1)
                high = both.astype(jnp.bfloat16)
                low = (both - high.astype(jnp.float32)).astype(jnp.bfloat16)
                right = jnp.concatenate([high, high, low], axis=0)
                left = jnp.concatenate([matrix[me_freq, mine, :], matrix[other_freq, mine, :]], axis=0)
                part = jnp.dot(left, right, preferred_element_type=jnp.float32)
                for k in range(2):
                    lanes = slice(k * LANES, (k + 1) * LANES)
                    own_part[pl.ds(start + 2 * pair + k, size, stride=ROWS), :] = part[:size, lanes]
                    send_part[pl.ds(start + 2 * ROWS + 2 * pair + k, size, stride=ROWS), :] = part[size:, lanes]
                return inner

            lax.fori_loop(0, ROWS // 2, mix, 0)
            swap(n).start()
        swap(0).wait_recv()

        other_energy = recv_part[slot, pl.ds(0, ROWS), :]
        other_moment = recv_part[slot, pl.ds(ROWS, ROWS), :]
        if last:
            swap(1).wait_recv()
            for j in range(1, dir_groups):
                last_copy(j, 1).wait_recv()
            energy, moment = lax.fori_loop(
                head, freq_local, functools.partial(refract, True), (energy, moment)
            )
            tail_send[pl.ds(0, ROWS), :] = energy
            tail_send[pl.ds(ROWS, ROWS), :] = moment
            tail_swap = pltpu.make_async_remote_copy(
                src_ref=tail_send,
                dst_ref=tail_recv,
                send_sem=tail_send_sem,
                recv_sem=tail_recv_sem,
                device_id={"freq": other_freq},
                device_id_type=MESH_ID,
            )
            tail_swap.start()
            tail_rows = dir_total * TAIL
            ours = pl.ds(pl.multiple_of(dir_first * freq_local, 16), bins)
            for side, held in enumerate((tail_send, tail_recv)):
                if side:
                    tail_swap.wait_recv()

                def mix_tail(pair, inner):
                    first = held[pl.ds(2 * ROWS + 2 * pair, tail_rows, stride=ROWS), :]
                    second = held[pl.ds(2 * ROWS + 2 * pair + 1, tail_rows, stride=ROWS), :]
                    both = jnp.concatenate([first, second], axis=1)
                    high = both.astype(jnp.bfloat16)
                    low = (both - high.astype(jnp.float32)).astype(jnp.bfloat16)
                    right = jnp.concatenate([high, high, low], axis=0)
                    left = tail_matrix[side, me_freq, ours, :]
                    part = jnp.dot(left, right, preferred_element_type=jnp.float32)
                    for k in range(2):
                        at = pl.ds(2 * pair + k, bins, stride=ROWS)
                        own_part[at, :] = own_part[at, :] + part[:, k * LANES : (k + 1) * LANES]
                    return inner

                lax.fori_loop(0, ROWS // 2, mix_tail, 0)
            other_energy = tail_recv[pl.ds(0, ROWS), :]
            other_moment = tail_recv[pl.ds(ROWS, ROWS), :]
            tail_swap.wait_send()

        sea = sea_ref[rows, cols]
        energy = (energy + other_energy) / bin_total
        moment = (moment + other_moment) / bin_total
        mean_sigma = moment / (energy + small_eps)
        steepness = energy * mean_sigma * mean_sigma
        white = whitecap_coef * (steepness * steepness)
        nonlinear = sea * (nonlinear_coef * (energy * energy))
        rate = sea * rate_ref[rows, cols]
        cos_w = coswind[rows, cols]
        sin_w = sinwind[rows, cols]
        classes = depth_ref[rows, cols]

        for n, (first_dir, last_dir) in enumerate(piece_ends):
            if n > 0 and not last:
                swap(n).wait_recv()

            def source(f, inner):
                sigma = sigma_ref[freq_first + f]
                friction = jnp.full((ROWS, LANES), fric_ref[0, freq_first + f], jnp.float32)
                for k in range(1, class_count):
                    friction = jnp.where(classes == k, fric_ref[k, freq_first + f], friction)
                keep = sea * (1.0 - white * sigma - friction)
                grow = rate * sigma
                for d in range(first_dir, last_dir):
                    spot = d * freq_local + f
                    at = pl.ds(pl.multiple_of(spot * ROWS, ROWS), ROWS)
                    there = pl.ds(pl.multiple_of((spot + 2) * ROWS, ROWS), ROWS)
                    whole = pl.ds(pl.multiple_of(((dir_first + d) * freq_local + f) * ROWS, ROWS), ROWS)
                    align = jnp.maximum(cos_ref[dir_first + d] * cos_w + sin_ref[dir_first + d] * sin_w, 0.0)
                    mixed = own_part[at, :] + recv_part[slot, there, :]
                    out_ref[spot, rows, cols] = turned_buf[whole, :] * (keep + grow * align) + nonlinear * mixed
                return inner

            lax.fori_loop(0, freq_local, source, 0)
        for n in range(len(piece_ends)):
            swap(n).wait_send()

    def run(c, carry):
        chunk(c, False)
        return carry

    lax.fori_loop(0, chunks - 1, run, 0)
    chunk(chunks - 1, True)

    def finish(c, carry):
        for j in range(1, dir_groups):
            dir_copy(c, j).wait_send()
        return carry

    lax.fori_loop(0, chunks - 1, finish, 0)
    for j in range(1, dir_groups):
        for n in range(2):
            last_copy(j, n).wait_send()


def shards(
    dir_groups,
    space_groups,
    spectrum,
    land_mask,
    depth_class,
    shift_count,
    turning,
    wind_rate,
    wind_angle,
    cfl,
    freq_turn,
    friction_table,
    transfer,
):
    dir_local, freq_local, row_count, col_count = spectrum.shape
    bins = dir_local * freq_local
    dir_total = dir_local * dir_groups
    freq_total = cfl.shape[0]
    angles = 2.0 * math.pi * np.arange(dir_total) / dir_total
    cosines = jnp.asarray(np.cos(angles), jnp.float32)
    sines = jnp.asarray(np.sin(angles), jnp.float32)
    sigmas = jnp.asarray(0.5 * np.power(1.07, np.arange(freq_total)), jnp.float32)
    chunks = (row_count // ROWS) * (col_count // LANES)
    depth = dir_total * freq_local
    peers = max(dir_groups - 1, 1)
    vmem = pl.BlockSpec(memory_space=pltpu.VMEM)
    hbm = pl.BlockSpec(memory_space=pltpu.HBM)
    shift_tiles = shift_count.shape[1]
    class_count = friction_table.shape[0]
    points = (row_count, col_count)
    f32 = jnp.float32
    evolved = pl.pallas_call(
        functools.partial(kernel, dir_groups, space_groups),
        out_shape=pltpu.VMEM((bins, row_count, col_count), f32),
        in_specs=[hbm] * 14,
        out_specs=vmem,
        scratch_shapes=[
            pltpu.VMEM(points, jnp.int32),
            pltpu.VMEM(points, jnp.int32),
            pltpu.VMEM((shift_tiles, row_count), jnp.int32),
            pltpu.VMEM(points, f32),
            pltpu.VMEM(points, f32),
            pltpu.VMEM(points, f32),
            pltpu.SMEM((freq_total,), f32),
            pltpu.SMEM((freq_total,), f32),
            pltpu.SMEM((class_count, freq_total), f32),
            pltpu.SMEM((dir_total,), f32),
            pltpu.SMEM((dir_total,), f32),
            pltpu.SMEM((freq_total,), f32),
            pltpu.SemaphoreType.DMA((12,)),
            pltpu.VMEM((bins * row_count, col_count), f32),
            pltpu.VMEM((chunks, dir_total, freq_local, ROWS, LANES), f32),
            pltpu.VMEM((depth * ROWS, LANES), f32),
            pltpu.VMEM((bins * ROWS, LANES), f32),
            pltpu.VMEM(((bins + 2) * ROWS, LANES), f32),
            pltpu.VMEM((2, (bins + 2) * ROWS, LANES), f32),
            pltpu.VMEM((2, depth, 3 * depth), jnp.bfloat16),
            pltpu.VMEM((dir_total, freq_local, transfer.shape[1]), f32),
            pltpu.VMEM((dir_total, ROWS, transfer.shape[1]), f32),
            pltpu.VMEM((2, 2, depth, 3 * dir_total * TAIL), jnp.bfloat16),
            pltpu.VMEM(((dir_total * TAIL + 2) * ROWS, LANES), f32),
            pltpu.VMEM(((dir_total * TAIL + 2) * ROWS, LANES), f32),
            pltpu.VMEM((bins, col_count), f32),
            pltpu.VMEM((bins, col_count), f32),
            pltpu.VMEM((bins, col_count), f32),
            pltpu.VMEM((bins, col_count), f32),
            pltpu.VMEM((row_count, col_count), f32),
            pltpu.VMEM((row_count, col_count), jnp.int32),
            pltpu.VMEM((row_count, col_count), f32),
            pltpu.VMEM((row_count, col_count), f32),
            pltpu.SemaphoreType.DMA((dir_local,)),
            pltpu.SemaphoreType.DMA,
            pltpu.SemaphoreType.DMA,
            pltpu.SemaphoreType.DMA,
            pltpu.SemaphoreType.DMA,
            pltpu.SemaphoreType.DMA((2,)),
            pltpu.SemaphoreType.DMA((2,)),
            pltpu.SemaphoreType.DMA((chunks + 1, peers)),
            pltpu.SemaphoreType.DMA((chunks + 1, peers)),
            pltpu.SemaphoreType.DMA((2, 2)),
            pltpu.SemaphoreType.DMA((2, 2)),
        ],
        compiler_params=pltpu.CompilerParams(
            collective_id=0, has_side_effects=True, vmem_limit_bytes=52 * 1024 * 1024
        ),
        name="wave_step",
    )(
        spectrum.reshape(bins * row_count, col_count),
        land_mask,
        depth_class,
        shift_count.T,
        turning,
        wind_rate,
        wind_angle,
        cfl,
        freq_turn,
        friction_table,
        cosines,
        sines,
        sigmas,
        transfer.reshape(dir_total, freq_total, transfer.shape[1]),
    )
    return evolved.reshape(spectrum.shape)


def solution(mesh):
    points = P(("groups", "space"), None)
    in_specs = (P("dir", "freq", ("groups", "space"), None),) + (points,) * 6 + (P(),) * 4
    return jax.shard_map(
        functools.partial(shards, mesh.shape["dir"], mesh.shape["space"]),
        mesh=mesh,
        in_specs=in_specs,
        out_specs=P("dir", "freq", ("groups", "space"), None),
        check_vma=False,
    )
```

```python
import functools
import math

import jax
import jax.numpy as jnp
import numpy as np
from jax import lax
from jax.experimental import pallas as pl
from jax.experimental.pallas import tpu as pltpu
from jax.sharding import PartitionSpec as P

ROWS = 8
LANES = 128
TAIL = 4
MESH_ID = pl.DeviceIdType.MESH

whitecap_coef = 0.01
nonlinear_coef = 0.5
small_eps = 1e-05


def kernel(
    dir_groups,
    space_groups,
    spectrum_ref,
    land_hbm,
    depth_hbm,
    shift_hbm,
    turning_hbm,
    rate_hbm,
    wind_hbm,
    cfl_hbm,
    turn_hbm,
    fric_hbm,
    cos_hbm,
    sin_hbm,
    sigma_hbm,
    transfer_ref,
    out_ref,
    land_ref,
    depth_ref,
    shift_ref,
    turning_ref,
    rate_ref,
    wind_ref,
    cfl_ref,
    turn_ref,
    fric_ref,
    cos_ref,
    sin_ref,
    sigma_ref,
    small_sem,
    spec_ref,
    grid_buf,
    turned_buf,
    own_part,
    send_part,
    recv_part,
    matrix,
    raw_matrix,
    raw_other,
    tail_matrix,
    tail_send,
    tail_recv,
    edge_top,
    edge_bot,
    halo_up,
    halo_dn,
    sea_ref,
    shift_wide,
    coswind,
    sinwind,
    spec_sem,
    matrix_sem,
    other_sem,
    tail_send_sem,
    tail_recv_sem,
    halo_send,
    halo_recv,
    dir_send,
    dir_recv,
    part_send,
    part_recv,
):
    me_dir = lax.axis_index("dir")
    me_space = lax.axis_index("space")
    me_freq = lax.axis_index("freq")
    other_freq = 1 - me_freq
    dir_total, freq_local = grid_buf.shape[1], grid_buf.shape[2]
    dir_local = dir_total // dir_groups
    bins = dir_local * freq_local
    row_count = out_ref.shape[1]
    col_count = out_ref.shape[2]
    tiles = row_count // ROWS
    halves = col_count // LANES
    chunks = tiles * halves
    class_count = fric_ref.shape[0]
    bin_total = transfer_ref.shape[2]
    dir_first = me_dir * dir_local
    freq_first = pl.multiple_of(me_freq * freq_local, 8)

    barrier = pltpu.get_barrier_semaphore()
    for j in range(1, dir_groups):
        pl.semaphore_signal(
            barrier, inc=1, device_id={"dir": lax.rem(me_dir + j, dir_groups)}, device_id_type=MESH_ID
        )
    pl.semaphore_signal(barrier, inc=1, device_id={"freq": other_freq}, device_id_type=MESH_ID)

    @pl.when(me_space > 0)
    def _():
        pl.semaphore_signal(barrier, inc=1, device_id={"space": me_space - 1}, device_id_type=MESH_ID)

    @pl.when(me_space < space_groups - 1)
    def _():
        pl.semaphore_signal(barrier, inc=1, device_id={"space": me_space + 1}, device_id_type=MESH_ID)

    small = [
        pltpu.make_async_copy(source, table, small_sem.at[n])
        for n, (source, table) in enumerate(
            (
                (land_hbm, land_ref),
                (cfl_hbm, cfl_ref),
                (cos_hbm, cos_ref),
                (sin_hbm, sin_ref),
                (turning_hbm, turning_ref),
                (turn_hbm, turn_ref),
                (fric_hbm, fric_ref),
                (sigma_hbm, sigma_ref),
                (depth_hbm, depth_ref),
                (shift_hbm, shift_ref),
                (rate_hbm, rate_ref),
                (wind_hbm, wind_ref),
            )
        )
    ]
    for copy in small:
        copy.start()

    def spec_copy(d):
        piece = pl.ds(pl.multiple_of(d * freq_local * row_count, ROWS), freq_local * row_count)
        return pltpu.make_async_copy(spectrum_ref.at[piece], spec_ref.at[piece], spec_sem.at[d])

    def start_copy(d, carry):
        spec_copy(d).start()
        return carry

    lax.fori_loop(0, dir_local, start_copy, 0)
    matrix_copy = pltpu.make_async_copy(
        transfer_ref.at[:, pl.ds(freq_first, freq_local), :], raw_matrix, matrix_sem
    )
    matrix_copy.start()
    other_copy = pltpu.make_async_copy(
        transfer_ref.at[:, pl.ds(pl.multiple_of(other_freq * freq_local + freq_local - ROWS, ROWS), ROWS), :],
        raw_other,
        other_sem,
    )
    other_copy.start()

    for copy in small[:4]:
        copy.wait()
    sea_ref[...] = jnp.where(land_ref[...] == 1, 1.0, 0.0)

    first_sea = sea_ref[pl.ds(0, ROWS), :]
    last_sea = sea_ref[pl.ds(row_count - ROWS, ROWS), :]

    def pack(b):
        base = pl.multiple_of(b * row_count, ROWS)
        top = spec_ref[pl.ds(base, ROWS), :] * first_sea
        low = spec_ref[pl.ds(base + row_count - ROWS, ROWS), :] * last_sea
        edge_top[pl.ds(b, 1), :] = top[:1]
        edge_bot[pl.ds(b, 1), :] = low[ROWS - 1 :]

    pl.semaphore_wait(
        barrier,
        dir_groups
        + (me_space > 0).astype(jnp.int32)
        + (me_space < space_groups - 1).astype(jnp.int32),
    )

    up_copy = pltpu.make_async_remote_copy(
        src_ref=edge_top,
        dst_ref=halo_dn,
        send_sem=halo_send.at[0],
        recv_sem=halo_recv.at[0],
        device_id={"space": jnp.maximum(me_space - 1, 0)},
        device_id_type=MESH_ID,
    )
    down_copy = pltpu.make_async_remote_copy(
        src_ref=edge_bot,
        dst_ref=halo_up,
        send_sem=halo_send.at[1],
        recv_sem=halo_recv.at[1],
        device_id={"space": jnp.minimum(me_space + 1, space_groups - 1)},
        device_id_type=MESH_ID,
    )

    head = freq_local - TAIL

    def dir_copy(c, j, first=0, count=dir_local, low=0, bands=freq_local, sem=None):
        sem = c if sem is None else sem
        region = grid_buf.at[c, pl.ds(dir_first + first, count), pl.ds(low, bands)]
        return pltpu.make_async_remote_copy(
            src_ref=region,
            dst_ref=region,
            send_sem=dir_send.at[sem, j - 1],
            recv_sem=dir_recv.at[sem, j - 1],
            device_id={"dir": lax.rem(me_dir + j, dir_groups)},
            device_id_type=MESH_ID,
        )

    def last_copy(j, n):
        if n == 0:
            return dir_copy(chunks - 1, j, low=0, bands=head)
        return dir_copy(chunks - 1, j, low=head, bands=TAIL, sem=chunks)

    row_id = lax.broadcasted_iota(jnp.int32, (ROWS, col_count), 0)
    col_id = lax.broadcasted_iota(jnp.int32, (ROWS, col_count), 1)

    def propagate(tile, place):
        sea = sea_ref[pl.ds(tile * ROWS, ROWS), :]
        if tile > 0:
            sea_prev = sea_ref[pl.ds(tile * ROWS - ROWS, ROWS), :]
        if tile < tiles - 1:
            sea_next = sea_ref[pl.ds(tile * ROWS + ROWS, ROWS), :]

        def per_dir(d, carry):
            if place == 0:
                spec_copy(d).wait()
            cos_d = cos_ref[dir_first + d]
            sin_d = sin_ref[dir_first + d]

            def per_freq(f, inner):
                b = d * freq_local + f
                if place == 0:
                    pack(b)
                base = pl.multiple_of(b * row_count, ROWS)
                here = spec_ref[pl.ds(base + tile * ROWS, ROWS), :] * sea
                if tile > 0:
                    prev = spec_ref[pl.ds(base + (tile - 1) * ROWS, ROWS), :] * sea_prev
                    above = pltpu.roll(jnp.where(row_id == ROWS - 1, prev, here), 1, 0)
                else:
                    above = jnp.where(row_id == 0, halo_up[pl.ds(b, 1), :], pltpu.roll(here, 1, 0))
                if tile < tiles - 1:
                    later = spec_ref[pl.ds(base + (tile + 1) * ROWS, ROWS), :] * sea_next
                    below = pltpu.roll(jnp.where(row_id == 0, later, here), ROWS - 1, 0)
                else:
                    below = jnp.where(
                        row_id == ROWS - 1, halo_dn[pl.ds(b, 1), :], pltpu.roll(here, ROWS - 1, 0)
                    )
                left = jnp.where(col_id == 0, 0.0, pltpu.roll(here, 1, 1))
                right = jnp.where(col_id == col_count - 1, 0.0, pltpu.roll(here, col_count - 1, 1))
                speed = cfl_ref[freq_first + f]
                speed_x = speed * cos_d
                speed_y = speed * sin_d
                moved = here - jnp.maximum(speed_x, 0.0) * (here - above)
                moved = moved - jnp.minimum(speed_x, 0.0) * (below - here)
                moved = moved - jnp.maximum(speed_y, 0.0) * (here - left)
                moved = moved - jnp.minimum(speed_y, 0.0) * (right - here)
                moved = moved * sea
                for h in range(halves):
                    grid_buf[place * halves + h, dir_first + d, f] = moved[:, h * LANES : (h + 1) * LANES]
                return inner

            lax.fori_loop(0, freq_local, per_freq, 0, unroll=4)
            if place == 0:
                for h in range(halves):
                    for j in range(1, dir_groups):
                        dir_copy(h, j, d, 1).start()
            return carry

        lax.fori_loop(0, dir_local, per_dir, 0)
        if place > 0:
            for h in range(halves):
                for j in range(1, dir_groups):
                    if place * halves + h == chunks - 1:
                        for n in range(2):
                            last_copy(j, n).start()
                    else:
                        dir_copy(place * halves + h, j).start()

    for place in range(tiles - 2):
        propagate(place + 1, place)

    @pl.when(me_space > 0)
    def _():
        up_copy.start()

    @pl.when(me_space < space_groups - 1)
    def _():
        down_copy.start()

    @pl.when(me_space > 0)
    def _():
        up_copy.wait_send()
        down_copy.wait_recv()

    @pl.when(me_space == 0)
    def _():
        halo_up[...] = jnp.zeros_like(halo_up)

    @pl.when(me_space < space_groups - 1)
    def _():
        down_copy.wait_send()
        up_copy.wait_recv()

    @pl.when(me_space == space_groups - 1)
    def _():
        halo_dn[...] = jnp.zeros_like(halo_dn)

    propagate(0, tiles - 2)
    propagate(tiles - 1, tiles - 1)

    for copy in small[4:]:
        copy.wait()
    coswind[...] = jnp.cos(wind_ref[...])
    sinwind[...] = jnp.sin(wind_ref[...])
    shift_tiles = shift_ref.shape[0]
    width = col_count // shift_tiles
    tile_of = lax.broadcasted_iota(jnp.int32, (shift_tiles, col_count), 1) // width
    tile_id = lax.broadcasted_iota(jnp.int32, (shift_tiles, col_count), 0)
    shift_wide[...] = lax.dot_general(
        shift_ref[...].astype(jnp.float32),
        (tile_of == tile_id).astype(jnp.float32),
        (((0,), (0,)), ((), ())),
        preferred_element_type=jnp.float32,
    ).astype(jnp.int32)

    matrix_copy.wait()
    other_copy.wait()
    depth = dir_total * freq_local
    for m in range(bin_total // LANES):
        block = raw_matrix[:, :, m * LANES : (m + 1) * LANES].reshape(depth, LANES)
        high = block.astype(jnp.bfloat16).astype(jnp.float32)
        low = block - high
        turned_block = jnp.concatenate([high, low, high], axis=0).T.astype(jnp.bfloat16)
        for piece in range(LANES // freq_local):
            d, g = divmod(m * (LANES // freq_local) + piece, 2)
            matrix[g, pl.ds(d * freq_local, freq_local), :] = turned_block[
                piece * freq_local : (piece + 1) * freq_local
            ]

    middle = (dir_local + 1) // 2
    piece_ends = ((0, middle), (middle, dir_local))

    eight = lax.broadcasted_iota(jnp.int32, (dir_total // 2, ROWS, LANES), 1)
    for m in range(bin_total // LANES):
        lanes = slice(m * LANES, (m + 1) * LANES)
        for side in range(2):
            block = raw_other[:, :, lanes] if side else raw_matrix[:, freq_local - ROWS :, lanes]
            pairs = block.reshape(dir_total // 2, 2, ROWS, LANES)
            block = jnp.where(eight < TAIL, pltpu.roll(pairs[:, 0], TAIL, 1), pairs[:, 1])
            block = block.reshape(dir_total * TAIL, LANES)
            high = block.astype(jnp.bfloat16).astype(jnp.float32)
            low = block - high
            turned_block = jnp.concatenate([high, low, high], axis=0).T.astype(jnp.bfloat16)
            for piece in range(LANES // freq_local):
                d, g = divmod(m * (LANES // freq_local) + piece, 2)
                tail_matrix[side, g, pl.ds(d * freq_local, freq_local), :] = turned_block[
                    piece * freq_local : (piece + 1) * freq_local
                ]

    def chunk(c, last):
        slot = c % 2
        pieces = ((0, dir_local),) if last else piece_ends
        if last:
            tile, half = tiles - 1, halves - 1
        else:
            place = c // halves
            half = c % halves
            tile = jnp.where(place < tiles - 2, place + 1, jnp.where(place == tiles - 2, 0, tiles - 1))
        rows = pl.ds(tile * ROWS if last else pl.multiple_of(tile * ROWS, ROWS), ROWS)
        cols = pl.ds(half * LANES if last else pl.multiple_of(half * LANES, LANES), LANES)
        for j in range(1, dir_groups):
            copy = last_copy(j, 0) if last else dir_copy(c, j)
            copy.wait_recv()

        shift = shift_wide[rows, cols]
        turning = turning_ref[rows, cols]
        picks = [shift == k for k in range(-2, 2)]

        def refract(in_tail, f, sums):
            weight = turning * turn_ref[freq_first + f]
            rest = 1.0 - weight
            moved = [grid_buf[c, d, f] for d in range(dir_total)]

            def shifted(d):
                result = moved[(d - 2) % dir_total]
                for k in (1, 0, -1, -2):
                    result = jnp.where(picks[k + 2], moved[(d - k) % dir_total], result)
                return result

            before = shifted(-1)
            total = jnp.zeros((ROWS, LANES), jnp.float32)
            for d in range(dir_total):
                now = shifted(d)
                turned = rest * now + weight * before
                turned_buf[pl.ds(pl.multiple_of((d * freq_local + f) * ROWS, ROWS), ROWS), :] = turned
                if in_tail:
                    spot = (d * TAIL + f - head + 2) * ROWS
                    tail_send[pl.ds(pl.multiple_of(spot, ROWS), ROWS), :] = turned
                total = total + turned
                before = now
            return sums[0] + total, sums[1] + total * sigma_ref[freq_first + f]

        zero = jnp.zeros((ROWS, LANES), jnp.float32)
        energy, moment = lax.fori_loop(
            0, head if last else freq_local, functools.partial(refract, False), (zero, zero)
        )
        if last:

            def clear(d, inner):
                spot = pl.multiple_of((d * freq_local + head) * ROWS, ROWS)
                turned_buf[pl.ds(spot, TAIL * ROWS), :] = jnp.zeros((TAIL * ROWS, LANES), jnp.float32)
                return inner

            lax.fori_loop(0, dir_total, clear, 0)
        send_part[pl.ds(0, ROWS), :] = energy
        send_part[pl.ds(ROWS, ROWS), :] = moment

        def swap(n):
            low, high = pieces[n]
            low = 0 if n == 0 else (low * freq_local + 2) * ROWS
            piece = pl.ds(low, (high * freq_local + 2) * ROWS - low)
            return pltpu.make_async_remote_copy(
                src_ref=send_part.at[piece],
                dst_ref=recv_part.at[slot, piece],
                send_sem=part_send.at[slot, n],
                recv_sem=part_recv.at[slot, n],
                device_id={"freq": other_freq},
                device_id_type=MESH_ID,
            )

        for n, (first_dir, last_dir) in enumerate(pieces):
            size = (last_dir - first_dir) * freq_local
            start = first_dir * freq_local * ROWS
            mine = pl.ds(pl.multiple_of((dir_first + first_dir) * freq_local, 16), size)

            def mix(pair, inner):
                first = turned_buf[pl.ds(2 * pair, depth, stride=ROWS), :]
                second = turned_buf[pl.ds(2 * pair + 1, depth, stride=ROWS), :]
                both = jnp.concatenate([first, second], axis=1)
                high = both.astype(jnp.bfloat16)
                low = (both - high.astype(jnp.float32)).astype(jnp.bfloat16)
                right = jnp.concatenate([high, high, low], axis=0)
                left = jnp.concatenate([matrix[me_freq, mine, :], matrix[other_freq, mine, :]], axis=0)
                part = jnp.dot(left, right, preferred_element_type=jnp.float32)
                for k in range(2):
                    lanes = slice(k * LANES, (k + 1) * LANES)
                    own_part[pl.ds(start + 2 * pair + k, size, stride=ROWS), :] = part[:size, lanes]
                    send_part[pl.ds(start + 2 * ROWS + 2 * pair + k, size, stride=ROWS), :] = part[size:, lanes]
                return inner

            lax.fori_loop(0, ROWS // 2, mix, 0)
            swap(n).start()
        if last:
            for j in range(1, dir_groups):
                last_copy(j, 1).wait_recv()
            energy, moment = lax.fori_loop(
                head, freq_local, functools.partial(refract, True), (energy, moment)
            )
            tail_send[pl.ds(0, ROWS), :] = energy
            tail_send[pl.ds(ROWS, ROWS), :] = moment
            tail_swap = pltpu.make_async_remote_copy(
                src_ref=tail_send,
                dst_ref=tail_recv,
                send_sem=tail_send_sem,
                recv_sem=tail_recv_sem,
                device_id={"freq": other_freq},
                device_id_type=MESH_ID,
            )
            tail_swap.start()
            tail_rows = dir_total * TAIL
            ours = pl.ds(pl.multiple_of(dir_first * freq_local, 16), bins)
            for side, held in enumerate((tail_send, tail_recv)):
                if side:
                    tail_swap.wait_recv()

                def mix_tail(pair, inner):
                    first = held[pl.ds(2 * ROWS + 2 * pair, tail_rows, stride=ROWS), :]
                    second = held[pl.ds(2 * ROWS + 2 * pair + 1, tail_rows, stride=ROWS), :]
                    both = jnp.concatenate([first, second], axis=1)
                    high = both.astype(jnp.bfloat16)
                    low = (both - high.astype(jnp.float32)).astype(jnp.bfloat16)
                    right = jnp.concatenate([high, high, low], axis=0)
                    left = tail_matrix[side, me_freq, ours, :]
                    part = jnp.dot(left, right, preferred_element_type=jnp.float32)
                    for k in range(2):
                        at = pl.ds(2 * pair + k, bins, stride=ROWS)
                        own_part[at, :] = own_part[at, :] + part[:, k * LANES : (k + 1) * LANES]
                    return inner

                lax.fori_loop(0, ROWS // 2, mix_tail, 0, unroll=True)
            other_energy = tail_recv[pl.ds(0, ROWS), :]
            other_moment = tail_recv[pl.ds(ROWS, ROWS), :]
            tail_swap.wait_send()
            swap(0).wait_recv()
        else:
            swap(0).wait_recv()
            other_energy = recv_part[slot, pl.ds(0, ROWS), :]
            other_moment = recv_part[slot, pl.ds(ROWS, ROWS), :]

        sea = sea_ref[rows, cols]
        energy = (energy + other_energy) / bin_total
        moment = (moment + other_moment) / bin_total
        mean_sigma = moment / (energy + small_eps)
        steepness = energy * mean_sigma * mean_sigma
        white = whitecap_coef * (steepness * steepness)
        nonlinear = sea * (nonlinear_coef * (energy * energy))
        rate = sea * rate_ref[rows, cols]
        cos_w = coswind[rows, cols]
        sin_w = sinwind[rows, cols]
        classes = depth_ref[rows, cols]

        for n, (first_dir, last_dir) in enumerate(pieces):
            if n > 0:
                swap(n).wait_recv()

            def source(f, inner):
                sigma = sigma_ref[freq_first + f]
                friction = jnp.full((ROWS, LANES), fric_ref[0, freq_first + f], jnp.float32)
                for k in range(1, class_count):
                    friction = jnp.where(classes == k, fric_ref[k, freq_first + f], friction)
                keep = sea * (1.0 - white * sigma - friction)
                grow = rate * sigma
                for d in range(first_dir, last_dir):
                    spot = d * freq_local + f
                    at = pl.ds(pl.multiple_of(spot * ROWS, ROWS), ROWS)
                    there = pl.ds(pl.multiple_of((spot + 2) * ROWS, ROWS), ROWS)
                    whole = pl.ds(pl.multiple_of(((dir_first + d) * freq_local + f) * ROWS, ROWS), ROWS)
                    align = jnp.maximum(cos_ref[dir_first + d] * cos_w + sin_ref[dir_first + d] * sin_w, 0.0)
                    mixed = own_part[at, :] + recv_part[slot, there, :]
                    out_ref[spot, rows, cols] = turned_buf[whole, :] * (keep + grow * align) + nonlinear * mixed
                return inner

            lax.fori_loop(0, freq_local, source, 0)
        for n in range(len(pieces)):
            swap(n).wait_send()

    def run(c, carry):
        chunk(c, False)
        return carry

    lax.fori_loop(0, chunks - 1, run, 0)
    chunk(chunks - 1, True)

    def finish(c, carry):
        for j in range(1, dir_groups):
            dir_copy(c, j).wait_send()
        return carry

    lax.fori_loop(0, chunks - 1, finish, 0)
    for j in range(1, dir_groups):
        for n in range(2):
            last_copy(j, n).wait_send()


def shards(
    dir_groups,
    space_groups,
    spectrum,
    land_mask,
    depth_class,
    shift_count,
    turning,
    wind_rate,
    wind_angle,
    cfl,
    freq_turn,
    friction_table,
    transfer,
):
    dir_local, freq_local, row_count, col_count = spectrum.shape
    bins = dir_local * freq_local
    dir_total = dir_local * dir_groups
    freq_total = cfl.shape[0]
    angles = 2.0 * math.pi * np.arange(dir_total) / dir_total
    cosines = jnp.asarray(np.cos(angles), jnp.float32)
    sines = jnp.asarray(np.sin(angles), jnp.float32)
    sigmas = jnp.asarray(0.5 * np.power(1.07, np.arange(freq_total)), jnp.float32)
    chunks = (row_count // ROWS) * (col_count // LANES)
    depth = dir_total * freq_local
    peers = max(dir_groups - 1, 1)
    vmem = pl.BlockSpec(memory_space=pltpu.VMEM)
    hbm = pl.BlockSpec(memory_space=pltpu.HBM)
    shift_tiles = shift_count.shape[1]
    class_count = friction_table.shape[0]
    points = (row_count, col_count)
    f32 = jnp.float32
    evolved = pl.pallas_call(
        functools.partial(kernel, dir_groups, space_groups),
        out_shape=pltpu.VMEM((bins, row_count, col_count), f32),
        in_specs=[hbm] * 14,
        out_specs=vmem,
        scratch_shapes=[
            pltpu.VMEM(points, jnp.int32),
            pltpu.VMEM(points, jnp.int32),
            pltpu.VMEM((shift_tiles, row_count), jnp.int32),
            pltpu.VMEM(points, f32),
            pltpu.VMEM(points, f32),
            pltpu.VMEM(points, f32),
            pltpu.SMEM((freq_total,), f32),
            pltpu.SMEM((freq_total,), f32),
            pltpu.SMEM((class_count, freq_total), f32),
            pltpu.SMEM((dir_total,), f32),
            pltpu.SMEM((dir_total,), f32),
            pltpu.SMEM((freq_total,), f32),
            pltpu.SemaphoreType.DMA((12,)),
            pltpu.VMEM((bins * row_count, col_count), f32),
            pltpu.VMEM((chunks, dir_total, freq_local, ROWS, LANES), f32),
            pltpu.VMEM((depth * ROWS, LANES), f32),
            pltpu.VMEM((bins * ROWS, LANES), f32),
            pltpu.VMEM(((bins + 2) * ROWS, LANES), f32),
            pltpu.VMEM((2, (bins + 2) * ROWS, LANES), f32),
            pltpu.VMEM((2, depth, 3 * depth), jnp.bfloat16),
            pltpu.VMEM((dir_total, freq_local, transfer.shape[1]), f32),
            pltpu.VMEM((dir_total, ROWS, transfer.shape[1]), f32),
            pltpu.VMEM((2, 2, depth, 3 * dir_total * TAIL), jnp.bfloat16),
            pltpu.VMEM(((dir_total * TAIL + 2) * ROWS, LANES), f32),
            pltpu.VMEM(((dir_total * TAIL + 2) * ROWS, LANES), f32),
            pltpu.VMEM((bins, col_count), f32),
            pltpu.VMEM((bins, col_count), f32),
            pltpu.VMEM((bins, col_count), f32),
            pltpu.VMEM((bins, col_count), f32),
            pltpu.VMEM((row_count, col_count), f32),
            pltpu.VMEM((row_count, col_count), jnp.int32),
            pltpu.VMEM((row_count, col_count), f32),
            pltpu.VMEM((row_count, col_count), f32),
            pltpu.SemaphoreType.DMA((dir_local,)),
            pltpu.SemaphoreType.DMA,
            pltpu.SemaphoreType.DMA,
            pltpu.SemaphoreType.DMA,
            pltpu.SemaphoreType.DMA,
            pltpu.SemaphoreType.DMA((2,)),
            pltpu.SemaphoreType.DMA((2,)),
            pltpu.SemaphoreType.DMA((chunks + 1, peers)),
            pltpu.SemaphoreType.DMA((chunks + 1, peers)),
            pltpu.SemaphoreType.DMA((2, 2)),
            pltpu.SemaphoreType.DMA((2, 2)),
        ],
        compiler_params=pltpu.CompilerParams(
            collective_id=0, has_side_effects=True, vmem_limit_bytes=52 * 1024 * 1024
        ),
        name="wave_step",
    )(
        spectrum.reshape(bins * row_count, col_count),
        land_mask,
        depth_class,
        shift_count.T,
        turning,
        wind_rate,
        wind_angle,
        cfl,
        freq_turn,
        friction_table,
        cosines,
        sines,
        sigmas,
        transfer.reshape(dir_total, freq_total, transfer.shape[1]),
    )
    return evolved.reshape(spectrum.shape)


def solution(mesh):
    points = P(("groups", "space"), None)
    in_specs = (P("dir", "freq", ("groups", "space"), None),) + (points,) * 6 + (P(),) * 4
    return jax.shard_map(
        functools.partial(shards, mesh.shape["dir"], mesh.shape["space"]),
        mesh=mesh,
        in_specs=in_specs,
        out_specs=P("dir", "freq", ("groups", "space"), None),
        check_vma=False,
    )
```
